32 devices in a mesh: tm: 8 (over z, y), batch: 4 (over x, core).
Axes of the slice: x: 2, y: 2, z: 4, core: 2. Of those that a mesh axis runs over, the one named last changes fastest.
Arguments:
- inputs: bfloat16 [256, 4, 128], P('tm', 'batch'), may hold values from -6 to 6
- h_start: float32 [4, 128], P('batch'), may hold values from -4 to 4
- in_weight: bfloat16 [128, 384], replicated, may hold values from -0.5 to 0.5
- rec_weight: float32 [128, 384], replicated, may hold values from -0.5 to 0.5
- update_bias: float32 [128], replicated, may hold values from -1 to 14
- reset_bias: float32 [128], replicated, may hold values from -4 to 4
- cand_bias: float32 [128], replicated, may hold values from -3 to 3
- rec_bias: float32 [128], replicated, may hold values from -3 to 3
Outputs:
- states: float32 [256, 4, 128], P('tm', 'batch')
- residual_norms: float32 [2], replicated
The draws below stay inside these ranges and needn't reach their ends.
All inputs are finite; a program needn't handle non-finite values.
Results may differ from the reference program's by a relative error of at most 0.0003.
Values sent between devices are 32-bit elements; how exact they have to be, the bound alone decides.
No kernel may reach another device: no remote copies, remote signals or barrier semaphores. Data moves between devices by JAX's collectives and lax.ppermute only.
A program may use at most 64 MiB of HBM per device.

```python
import math
import jax
import jax.numpy as jnp
from jax import lax

H = 128
DIN = 128
STEPS_DEV = 32
ITERS = 2
BATCH = 4
TOTAL = 256


def draw_update_bias(key, part):
    key_pick = jax.random.fold_in(key, 11)
    key_slow = jax.random.fold_in(key, 12)
    key_fast = jax.random.fold_in(key, 13)
    key_middle = jax.random.fold_in(key, 14)
    slow_cut = 7
    middle_cut = 14
    kinds = jax.random.randint(key_pick, (H,), 0, 20)
    slow_bias = math.log(TOTAL) + jax.random.uniform(key_slow, (H,), jnp.float32, -0.5, 1.0)
    middle_bias = math.log(STEPS_DEV) + jax.random.uniform(key_middle, (H,), jnp.float32, 0.0, 2.5)
    fast_bias = jax.random.uniform(key_fast, (H,), jnp.float32, -1.0, 3.0)
    chosen = jnp.where(kinds < slow_cut, slow_bias, jnp.where(kinds < middle_cut, middle_bias, fast_bias))
    return chosen.astype(jnp.float32)


def levels(own_key, dims, shards, least, high):
    gain, own = 1.0, jax.random.fold_in(own_key, 6)
    for dim, shards_of in shards:
        heights = jnp.exp(jax.random.uniform(jax.random.fold_in(own, dim), (shards_of,), jnp.float32, least / len(shards), high / len(shards)))
        gain = gain * jnp.repeat(heights, dims[dim] // shards_of).reshape([-1 if axis == dim else 1 for axis in range(len(dims))])
    return gain


def gaussian(stream_key, shape, scale, most, cuts=(), kind=jnp.bfloat16):
    result = jax.random.normal(stream_key, shape, jnp.float32) * scale
    if len(cuts) > 0:
        result = levels(stream_key, shape, cuts, -0.22, 0.18) * result
    return jnp.clip(result, min=-most, max=most).astype(kind)


def setup_inputs(seed: int = 0) -> dict:
    keys = jax.random.split(jax.random.key(seed), 9)
    inputs = gaussian(keys[0], (TOTAL, BATCH, DIN), 1.0, 6.0, ((0, 8), (1, 4)))
    h_start = gaussian(keys[1], (BATCH, H), 0.5, 4.0, ((0, 4),), jnp.float32)
    in_weight = gaussian(keys[2], (DIN, 3 * H), DIN ** -0.5, 0.5)
    rec_weight = gaussian(keys[3], (H, 3 * H), H ** -0.5, 0.5, (), jnp.float32)
    update_bias = draw_update_bias(jax.random.fold_in(keys[8], 71), 0)
    reset_bias = gaussian(keys[5], (H,), 1.0, 4.0, (), jnp.float32)
    cand_bias = gaussian(keys[6], (H,), 0.5, 3.0, (), jnp.float32)
    rec_bias = gaussian(keys[7], (H,), 0.5, 3.0, (), jnp.float32)
    return {"inputs": inputs, "h_start": h_start, "in_weight": in_weight, "rec_weight": rec_weight, "update_bias": update_bias, "reset_bias": reset_bias, "cand_bias": cand_bias, "rec_bias": rec_bias}


HIGH = lax.Precision.HIGHEST

def cell_parts(in_gates, previous, rec_weight, update_bias, reset_bias, cand_bias, rec_bias):
    units = rec_weight.shape[0]
    rec_gates = jnp.dot(previous, rec_weight, precision=HIGH)
    update_gate = jax.nn.sigmoid(in_gates[:, :units] + rec_gates[:, :units] + update_bias)
    reset_gate = jax.nn.sigmoid(in_gates[:, units:2 * units] + rec_gates[:, units:2 * units] + reset_bias)
    recur_term = rec_gates[:, 2 * units:] + rec_bias
    candidate = jnp.tanh(in_gates[:, 2 * units:] + cand_bias + reset_gate * recur_term)
    stepped = (1.0 - update_gate) * candidate + update_gate * previous
    return (update_gate, reset_gate, recur_term, candidate, stepped)

def jacobian(previous, update_gate, reset_gate, recur_term, candidate, rec_weight, identity):
    units = rec_weight.shape[0]
    coef_update = (previous - candidate) * update_gate * (1.0 - update_gate)
    common = (1.0 - update_gate) * (1.0 - candidate * candidate)
    coef_cand = common * reset_gate
    coef_reset = common * recur_term * reset_gate * (1.0 - reset_gate)
    return identity * update_gate[..., None, :] + rec_weight[:, :units] * coef_update[..., None, :] + rec_weight[:, units:2 * units] * coef_reset[..., None, :] + rec_weight[:, 2 * units:] * coef_cand[..., None, :]

def reference(inputs, h_start, in_weight, rec_weight, update_bias, reset_bias, cand_bias, rec_bias):
    units = rec_weight.shape[0]
    identity = jnp.eye(units, dtype=jnp.float32)
    weights = (jnp.arange(TOTAL).astype(jnp.float32) + 1.0) / TOTAL
    sums = [jnp.zeros((), jnp.float32) for newton in range(ITERS)]
    results = []
    for sequence in range(BATCH):
        in_gates = jnp.dot(inputs[:, sequence, :], in_weight, preferred_element_type=jnp.float32)
        start = h_start[sequence]
        previous = jnp.zeros((TOTAL, units), jnp.float32).at[0].set(start)
        current = previous
        for newton in range(ITERS):
            parts = cell_parts(in_gates, previous, rec_weight, update_bias, reset_bias, cand_bias, rec_bias)
            if newton > 0:
                sums[newton - 1] = sums[newton - 1] + jnp.sum(weights[:, None] * (current - parts[4]) ** 2)

            def advance(carried, item):
                prev_row, gate_z, gate_r, recur_row, cand_row, step_row = item
                matrix = jacobian(prev_row, gate_z, gate_r, recur_row, cand_row, rec_weight, identity)
                offset = step_row - jnp.dot(prev_row, matrix, precision=HIGH)
                carried = jnp.dot(carried, matrix, precision=HIGH) + offset
                return (carried, carried)
            final_row, current = lax.scan(advance, start, (previous,) + tuple(parts))
            previous = jnp.concatenate([start[None, :], current[:-1]], axis=0)
        parts = cell_parts(in_gates, previous, rec_weight, update_bias, reset_bias, cand_bias, rec_bias)
        sums[ITERS - 1] = sums[ITERS - 1] + jnp.sum(weights[:, None] * (current - parts[4]) ** 2)
        results.append(current)
    states = jnp.stack(results, axis=1)
    denom = BATCH * units * (TOTAL + 1) / 2.0
    residual_norms = jnp.sqrt(jnp.stack(sums) / denom + 1e-06)
    return (states, residual_norms)
```

```python
import functools

import jax
import jax.numpy as jnp
from jax import lax
from jax.experimental import pallas as pl
from jax.experimental.pallas import tpu as pltpu
from jax.sharding import PartitionSpec as P

ITERS = 2
BLOCK = 4
WINDOW = 4
PAD = 16
F32 = jnp.float32
BF16 = jnp.bfloat16


def halves(value):
    high = value.astype(BF16)
    return high, (value - high.astype(F32)).astype(BF16)


def paired_rows(value):
    return jnp.concatenate(halves(value), axis=1)


def paired_cols(value):
    both = jnp.concatenate(halves(value), axis=1)
    return jnp.concatenate([both, both], axis=0)


def product(rows, cols):
    width = cols.shape[1]
    both = jnp.dot(paired_rows(rows), paired_cols(cols), preferred_element_type=F32)
    return both[:, :width] + both[:, width:]


def as_column(row):
    units = row.shape[1]
    return jnp.broadcast_to(row, (units, units)).T


def row_times(column, matrix):
    return jnp.sum(column * matrix, axis=0, keepdims=True)


def cell(gates, previous, rec_weight, rec_bias):
    units = previous.shape[1]
    rec = product(previous, rec_weight)
    update = jax.nn.sigmoid(gates[:, :units] + rec[:, :units])
    reset = jax.nn.sigmoid(gates[:, units : 2 * units] + rec[:, units : 2 * units])
    recur = rec[:, 2 * units :] + rec_bias
    cand = jnp.tanh(gates[:, 2 * units :] + reset * recur)
    stepped = (1.0 - update) * cand + update * previous
    return update, reset, recur, cand, stepped


def entering_state(first, maps):
    mine = lax.axis_index("tm")
    state = first
    for back in range(len(maps), 0, -1):
        state = jnp.where(mine >= back, through(state, maps[back - 1]), state)
    return state


def through(state, one_map):
    units = state.shape[1]
    column = as_column(state - one_map[units + 1 : units + 2, :])
    return row_times(column, one_map[:units, :]) + one_map[units : units + 1, :]


def fold(parts, prev_ref, weight_ref, coef_refs, mats_ref, vecs_ref, map_ref):
    update, reset, recur, cand, stepped = parts
    steps, units = update.shape
    previous = prev_ref[...]
    update_ref, coef_update_ref, coef_reset_ref, coef_cand_ref, step_ref = coef_refs
    common = (1.0 - update) * (1.0 - cand * cand)
    update_ref[...] = update
    coef_update_ref[...] = (previous - cand) * update * (1.0 - update)
    coef_reset_ref[...] = common * recur * reset * (1.0 - reset)
    coef_cand_ref[...] = common * reset
    step_ref[...] = stepped
    row = lax.broadcasted_iota(jnp.int32, (units, units), 0)
    col = lax.broadcasted_iota(jnp.int32, (units, units), 1)

    def slope(t):
        return (
            weight_ref[:, :units] * coef_update_ref[t : t + 1, :]
            + weight_ref[:, units : 2 * units] * coef_reset_ref[t : t + 1, :]
            + weight_ref[:, 2 * units :] * coef_cand_ref[t : t + 1, :]
        )

    def stacked(mat, vec):
        return jnp.concatenate([mat, jnp.broadcast_to(vec, (PAD, units))], axis=0)

    blocks = steps // BLOCK
    for inner in range(BLOCK):
        for block in range(blocks):
            t = block * BLOCK + inner
            keep = update_ref[t : t + 1, :]
            if inner == 0:
                mat = slope(t) + jnp.where(row == col, keep, 0.0)
                vec = step_ref[t : t + 1, :]
            else:
                before = stacked(mats_ref[t - 1], vecs_ref[t - 1 : t, :] - prev_ref[t : t + 1, :])
                after = product(before, slope(t)) + before * keep
                mat = after[:units]
                vec = after[units : units + 1] + step_ref[t : t + 1, :]
            mats_ref[t] = mat
            vecs_ref[t : t + 1, :] = vec

    items = [(b * BLOCK, (b + 1) * BLOCK - 1) for b in range(blocks)]
    free = steps
    while len(items) > 1:
        joined = []
        for (first, early), (second, late) in zip(items[0::2], items[1::2]):
            before = stacked(mats_ref[early], vecs_ref[early : early + 1, :] - prev_ref[second : second + 1, :])
            after = product(before, mats_ref[late])
            mats_ref[free] = after[:units]
            vecs_ref[free : free + 1, :] = after[units : units + 1] + vecs_ref[late : late + 1, :]
            joined.append((first, free))
            free += 1
        items = joined
    last = items[0][1]
    map_ref[:units, :] = mats_ref[last]
    map_ref[units : units + 1, :] = vecs_ref[last : last + 1, :]
    map_ref[units + 1 : units + 2, :] = prev_ref[0:1, :]
    map_ref[units + 2 :, :] = jnp.zeros((6, units), F32)


def unfold(entering, prev_ref, mats_ref, vecs_ref, out_ref):
    steps = prev_ref.shape[0]
    blocks = steps // BLOCK
    starts = {0: entering}
    slots = {(b, 1): (b + 1) * BLOCK - 1 for b in range(blocks)}
    free, span = steps, 2
    while span <= blocks:
        for b in range(0, blocks, span):
            slots[(b, span)] = free
            free += 1
        span *= 2
    columns = {}
    for b in range(blocks):
        pass
    order = sorted(range(blocks), key=lambda b: (bin(b).count("1"), b))
    for b in order:
        t = b * BLOCK
        column = as_column(starts[b] - prev_ref[t : t + 1, :])
        span = 2
        while b % span == 0 and b + span < blocks:
            slot = slots[(b, span)]
            starts[b + span] = row_times(column, mats_ref[slot]) + vecs_ref[slot : slot + 1, :]
            span *= 2
        for inner in range(BLOCK):
            state = row_times(column, mats_ref[t + inner]) + vecs_ref[t + inner : t + inner + 1, :]
            out_ref[t + inner : t + inner + 1, :] = state
        if b % 2 == 0 and b + 1 < blocks:
            starts[b + 1] = state


def shift_in(entering, states_ref, prev_ref):
    steps = states_ref.shape[0]
    prev_ref[0:1, :] = entering
    prev_ref[1:steps, :] = states_ref[0 : steps - 1, :]


def weighted_square(states, stepped):
    steps = states.shape[0]
    mine, count = lax.axis_index("tm"), lax.axis_size("tm")
    position = mine * steps + lax.broadcasted_iota(jnp.int32, states.shape, 0)
    weights = (position.astype(F32) + 1.0) / (steps * count)
    return jnp.sum(weights * (states - stepped) ** 2, axis=(0, 1), keepdims=True)


def first_kernel(
    inputs_ref, start_ref, in_weight_ref, weight_ref, update_bias_ref, reset_bias_ref,
    cand_bias_ref, rec_bias_ref,
    gates_ref, prev_ref, mats_ref, vecs_ref, map_ref, *coef_refs
):
    steps, units = prev_ref.shape
    gates = jnp.dot(inputs_ref[...], in_weight_ref[...], preferred_element_type=F32)
    bias = jnp.concatenate([update_bias_ref[...], reset_bias_ref[...], cand_bias_ref[...]], axis=1)
    gates = gates + bias
    gates_ref[...] = gates
    at_start = (lax.axis_index("tm") == 0) & (lax.broadcasted_iota(jnp.int32, (steps, units), 0) == 0)
    previous = jnp.where(at_start, start_ref[...], 0.0)
    prev_ref[...] = previous
    parts = cell(gates, previous, weight_ref[...], rec_bias_ref[...])
    fold(parts, prev_ref, weight_ref, coef_refs, mats_ref, vecs_ref, map_ref)


def hop_kernel(start_ref, arrived_ref, map_ref, *refs):
    maps, sent_ref = refs[:-1], refs[-1]
    first = jnp.where(lax.axis_index("tm") < WINDOW, start_ref[...], arrived_ref[0:1, :])
    state = through(entering_state(first, maps), map_ref)
    sent_ref[...] = jnp.broadcast_to(state, sent_ref.shape)


def next_kernel(
    last, near, start_ref, arrived_ref, gates_ref, old_prev_ref, old_mats_ref, old_vecs_ref, weight_ref,
    rec_bias_ref, sums_ref, *refs
):
    maps, refs = refs[:near], refs[near:]
    if last:
        states_ref, new_sums_ref, prev_ref = refs
    else:
        new_sums_ref, prev_ref, mats_ref, vecs_ref, map_ref, states_ref, *coef_refs = refs
    first = jnp.where(lax.axis_index("tm") < WINDOW, start_ref[...], arrived_ref[0:1, :])
    entering = entering_state(first, maps)
    unfold(entering, old_prev_ref, old_mats_ref, old_vecs_ref, states_ref)
    shift_in(entering, states_ref, prev_ref)
    parts = cell(gates_ref[...], prev_ref[...], weight_ref[...], rec_bias_ref[...])
    done = weighted_square(states_ref[...], parts[4])
    row = lax.broadcasted_iota(jnp.int32, sums_ref.shape, 0)
    new_sums_ref[...] = jnp.where(row == (1 if last else 0), done, sums_ref[...])
    if not last:
        fold(parts, prev_ref, weight_ref, coef_refs, mats_ref, vecs_ref, map_ref)


def call(kernel, args, outs, scratch=(), flops=0):
    return pl.pallas_call(
        kernel,
        out_shape=[jax.ShapeDtypeStruct(shape, F32) for shape in outs],
        in_specs=[pl.BlockSpec(memory_space=pltpu.VMEM)] * len(args),
        out_specs=[pl.BlockSpec(memory_space=pltpu.VMEM)] * len(outs),
        scratch_shapes=[pltpu.VMEM(shape, F32) for shape in scratch],
        compiler_params=pltpu.CompilerParams(vmem_limit_bytes=32 * 1024 * 1024),
    )(*args)


def shifted(value, by):
    count = lax.axis_size("tm")
    return lax.ppermute(value, "tm", [(i, i + by) for i in range(count - by)])


def summed(value):
    for axis in ("batch", "tm"):
        count, by = lax.axis_size(axis), 1
        while by < count:
            value = value + lax.ppermute(value, axis, [(i, i ^ by) for i in range(count)])
            by *= 2
    return value


def carry(start, own_map):
    count = lax.axis_size("tm")
    units = start.shape[1]
    maps = [shifted(own_map, back) for back in range(1, min(WINDOW, count))]
    arrived = jnp.zeros((8, units), F32)
    for hop in range(-(-count // WINDOW) - 1):
        (sent,) = call(hop_kernel, [start, arrived, own_map, *maps], [(8, units)])
        arrived = shifted(sent, WINDOW)
    return arrived, maps


def per_device(
    inputs, h_start, in_weight, rec_weight, update_bias, reset_bias, cand_bias, rec_bias
):
    steps, sequences = inputs.shape[0], inputs.shape[1]
    units = rec_weight.shape[0]
    row = lambda value: value.reshape(1, units)
    start = h_start
    slots = steps + steps // BLOCK
    rows = (steps, units)
    fold_outs = [rows, (slots, units, units), (slots, units), (units + 8, units)]
    coefs = [rows] * 5
    gates, prev, mats, vecs, own_map = call(
        first_kernel,
        [inputs.reshape(steps, -1), start, in_weight, rec_weight, row(update_bias), row(reset_bias),
         row(cand_bias), row(rec_bias)],
        [(steps, 3 * units)] + fold_outs,
        coefs,
    )
    sums = jnp.zeros((8, units), F32)
    for newton in range(ITERS):
        last = newton == ITERS - 1
        arrived, maps = carry(start, own_map)
        args = [start, arrived, gates, prev, mats, vecs, rec_weight, row(rec_bias), sums, *maps]
        kernel = functools.partial(next_kernel, last, len(maps))
        if last:
            states, sums = call(kernel, args, [rows, (8, units)], [rows])
        else:
            sums, prev, mats, vecs, own_map = call(
                kernel, args, [(8, units)] + fold_outs, [rows] + coefs
            )
    totals = summed(sums)[:ITERS, 0]
    denom = lax.axis_size("batch") * sequences * units * (steps * lax.axis_size("tm") + 1) / 2.0
    residual_norms = jnp.sqrt(totals / denom + 1e-06)
    return (states.reshape(steps, sequences, units), residual_norms)


def solution(mesh):
    in_specs = (P("tm", "batch", None), P("batch", None), P(), P(), P(), P(), P(), P())
    out_specs = (P("tm", "batch", None), P())
    return jax.shard_map(
        per_device, mesh=mesh, in_specs=in_specs, out_specs=out_specs, check_vma=False
    )
```

```python
import functools

import jax
import jax.numpy as jnp
from jax import lax
from jax.experimental import pallas as pl
from jax.experimental.pallas import tpu as pltpu
from jax.sharding import PartitionSpec as P

ITERS = 2
BLOCK = 4
WINDOW = 4
PAD = 16
F32 = jnp.float32
BF16 = jnp.bfloat16


def halves(value):
    high = value.astype(BF16)
    return high, (value - high.astype(F32)).astype(BF16)


def paired_rows(value):
    return jnp.concatenate(halves(value), axis=1)


def paired_cols(value):
    both = jnp.concatenate(halves(value), axis=1)
    return jnp.concatenate([both, both], axis=0)


def product(rows, cols):
    width = cols.shape[1]
    both = jnp.dot(paired_rows(rows), paired_cols(cols), preferred_element_type=F32)
    return both[:, :width] + both[:, width:]


def as_column(row):
    units = row.shape[1]
    return jnp.broadcast_to(row, (units, units)).T


def row_times(column, matrix):
    return jnp.sum(column * matrix, axis=0, keepdims=True)


def cell(gates, previous, rec_weight, rec_bias):
    units = previous.shape[1]
    rec = product(previous, rec_weight)
    update = jax.nn.sigmoid(gates[:, :units] + rec[:, :units])
    reset = jax.nn.sigmoid(gates[:, units : 2 * units] + rec[:, units : 2 * units])
    recur = rec[:, 2 * units :] + rec_bias
    cand = jnp.tanh(gates[:, 2 * units :] + reset * recur)
    stepped = (1.0 - update) * cand + update * previous
    return update, reset, recur, cand, stepped


def walk(first, refs, place, stop):
    state = first
    for other in range(stop):
        state = through(state, refs[place ^ other])
    return state


def group_start(consts_ref, arrived_refs):
    start = consts_ref[0:1, :]
    if not arrived_refs:
        return start
    return jnp.where(lax.axis_index("tm") < WINDOW, start, arrived_refs[0][0:1, :])


def through(state, one_map):
    units = state.shape[1]
    column = as_column(state - one_map[units + 1 : units + 2, :])
    return row_times(column, one_map[:units, :]) + one_map[units : units + 1, :]


def fold(parts, prev_ref, weight_ref, coef_refs, mats_ref, vecs_ref, map_ref):
    update, reset, recur, cand, stepped = parts
    steps, units = update.shape
    previous = prev_ref[...]
    update_ref, coef_update_ref, coef_reset_ref, coef_cand_ref, step_ref = coef_refs
    common = (1.0 - update) * (1.0 - cand * cand)
    update_ref[...] = update
    coef_update_ref[...] = (previous - cand) * update * (1.0 - update)
    coef_reset_ref[...] = common * recur * reset * (1.0 - reset)
    coef_cand_ref[...] = common * reset
    step_ref[...] = stepped
    row = lax.broadcasted_iota(jnp.int32, (units, units), 0)
    col = lax.broadcasted_iota(jnp.int32, (units, units), 1)

    def slope(t):
        return (
            weight_ref[:, :units] * coef_update_ref[t : t + 1, :]
            + weight_ref[:, units : 2 * units] * coef_reset_ref[t : t + 1, :]
            + weight_ref[:, 2 * units :] * coef_cand_ref[t : t + 1, :]
        )

    def stacked(mat, vec):
        return jnp.concatenate([mat, jnp.broadcast_to(vec, (PAD, units))], axis=0)

    blocks = steps // BLOCK
    for inner in range(BLOCK):
        for block in range(blocks):
            t = block * BLOCK + inner
            keep = update_ref[t : t + 1, :]
            if inner == 0:
                mat = slope(t) + jnp.where(row == col, keep, 0.0)
                vec = step_ref[t : t + 1, :]
            else:
                before = stacked(mats_ref[t - 1], vecs_ref[t - 1 : t, :] - prev_ref[t : t + 1, :])
                after = product(before, slope(t)) + before * keep
                mat = after[:units]
                vec = after[units : units + 1] + step_ref[t : t + 1, :]
            mats_ref[t] = mat
            vecs_ref[t : t + 1, :] = vec

    items = [(b * BLOCK, (b + 1) * BLOCK - 1) for b in range(blocks)]
    free = steps
    while len(items) > 1:
        joined = []
        for (first, early), (second, late) in zip(items[0::2], items[1::2]):
            before = stacked(mats_ref[early], vecs_ref[early : early + 1, :] - prev_ref[second : second + 1, :])
            after = product(before, mats_ref[late])
            mats_ref[free] = after[:units]
            vecs_ref[free : free + 1, :] = after[units : units + 1] + vecs_ref[late : late + 1, :]
            joined.append((first, free))
            free += 1
        items = joined
    last = items[0][1]
    map_ref[:units, :] = mats_ref[last]
    map_ref[units : units + 1, :] = vecs_ref[last : last + 1, :]
    map_ref[units + 1 : units + 2, :] = prev_ref[0:1, :]
    map_ref[units + 2 :, :] = jnp.zeros((6, units), F32)


def unfold(entering, prev_ref, mats_ref, vecs_ref, out_ref):
    steps = prev_ref.shape[0]
    blocks = steps // BLOCK
    starts = {0: entering}
    slots = {(b, 1): (b + 1) * BLOCK - 1 for b in range(blocks)}
    free, span = steps, 2
    while span <= blocks:
        for b in range(0, blocks, span):
            slots[(b, span)] = free
            free += 1
        span *= 2
    order = sorted(range(blocks), key=lambda b: (bin(b).count("1"), b))
    for b in order:
        t = b * BLOCK
        column = as_column(starts[b] - prev_ref[t : t + 1, :])
        span = 2
        while b % span == 0 and b + span < blocks:
            slot = slots[(b, span)]
            starts[b + span] = row_times(column, mats_ref[slot]) + vecs_ref[slot : slot + 1, :]
            span *= 2
        for inner in range(BLOCK):
            state = row_times(column, mats_ref[t + inner]) + vecs_ref[t + inner : t + inner + 1, :]
            out_ref[t + inner : t + inner + 1, :] = state
        if b % 2 == 0 and b + 1 < blocks:
            starts[b + 1] = state


def shift_in(entering, states_ref, prev_ref):
    steps = states_ref.shape[0]
    prev_ref[0:1, :] = entering
    prev_ref[1:steps, :] = states_ref[0 : steps - 1, :]


def weighted_square(states, stepped):
    steps = states.shape[0]
    mine, count = lax.axis_index("tm"), lax.axis_size("tm")
    position = mine * steps + lax.broadcasted_iota(jnp.int32, states.shape, 0)
    weights = (position.astype(F32) + 1.0) / (steps * count)
    return jnp.sum(weights * (states - stepped) ** 2, axis=(0, 1), keepdims=True)


def first_kernel(
    inputs_hbm, start_hbm, in_weight_hbm, weight_hbm, update_bias_hbm, reset_bias_hbm, cand_bias_hbm,
    rec_bias_hbm,
    gates_ref, prev_ref, mats_ref, vecs_ref, map_ref, weight_ref, consts_ref,
    inputs_ref, in_weight_ref, bias_ref, start_ref, rec_bias_ref, sems, *coef_refs
):
    steps, units = prev_ref.shape
    moves = [
        (inputs_hbm, inputs_ref), (in_weight_hbm, in_weight_ref), (weight_hbm, weight_ref),
        (update_bias_hbm, bias_ref.at[:, pl.ds(0, units)]),
        (reset_bias_hbm, bias_ref.at[:, pl.ds(units, units)]),
        (cand_bias_hbm, bias_ref.at[:, pl.ds(2 * units, units)]),
        (start_hbm, start_ref), (rec_bias_hbm, rec_bias_ref),
    ]
    copies = [pltpu.make_async_copy(src, dst, sems.at[i]) for i, (src, dst) in enumerate(moves)]
    for copy in copies:
        copy.start()
    for copy in copies:
        copy.wait()
    consts_ref[0:1, :] = start_ref[...]
    consts_ref[1:2, :] = rec_bias_ref[...]
    consts_ref[2:, :] = jnp.zeros((6, units), F32)
    gates = jnp.dot(inputs_ref[...], in_weight_ref[...], preferred_element_type=F32) + bias_ref[...]
    gates_ref[...] = gates
    at_start = (lax.axis_index("tm") == 0) & (lax.broadcasted_iota(jnp.int32, (steps, units), 0) == 0)
    previous = jnp.where(at_start, start_ref[...], 0.0)
    prev_ref[...] = previous
    parts = cell(gates, previous, weight_ref[...], rec_bias_ref[...])
    fold(parts, prev_ref, weight_ref, coef_refs, mats_ref, vecs_ref, map_ref)


def hop_kernel(held, consts_ref, *refs):
    maps, arrived, sent_ref = refs[:held], refs[held:-1], refs[-1]
    first = group_start(consts_ref, arrived)
    place = lax.rem(lax.axis_index("tm"), held)
    for mine in range(held):

        @pl.when(place == mine)
        def _():
            state = walk(first, maps, mine, held)
            sent_ref[...] = jnp.broadcast_to(state, sent_ref.shape)


def next_kernel(newton, held, hops, *refs):
    last = newton == ITERS - 1
    consts_ref, gates_ref, old_prev_ref, old_mats_ref, old_vecs_ref, weight_ref = refs[:6]
    maps, refs = refs[6 : 6 + held], refs[6 + held :]
    arrived, refs = refs[: min(hops, 1)], refs[min(hops, 1) :]
    if newton > 0:
        sums_ref, refs = refs[0], refs[1:]
    if last:
        states_ref, new_sums_ref, prev_ref, enter_ref = refs
    else:
        new_sums_ref, prev_ref, mats_ref, vecs_ref, map_ref, states_ref, enter_ref, *coef_refs = refs
    first = group_start(consts_ref, arrived)
    place = lax.rem(lax.axis_index("tm"), held)
    for mine in range(held):

        @pl.when(place == mine)
        def _():
            enter_ref[...] = walk(first, maps, mine, mine)

    entering = enter_ref[...]
    unfold(entering, old_prev_ref, old_mats_ref, old_vecs_ref, states_ref)
    shift_in(entering, states_ref, prev_ref)
    parts = cell(gates_ref[...], prev_ref[...], weight_ref[...], consts_ref[1:2, :])
    done = weighted_square(states_ref[...], parts[4])
    row = lax.broadcasted_iota(jnp.int32, new_sums_ref.shape, 0)
    new_sums_ref[...] = jnp.where(row == newton, done, sums_ref[...] if newton > 0 else 0.0)
    if not last:
        fold(parts, prev_ref, weight_ref, coef_refs, mats_ref, vecs_ref, map_ref)


def call(kernel, args, outs, scratch=(), space=pltpu.VMEM):
    args = [pltpu.with_memory_space_constraint(arg, space) for arg in args]
    return pl.pallas_call(
        kernel,
        out_shape=[jax.ShapeDtypeStruct(shape, F32) for shape in outs],
        in_specs=[pl.BlockSpec(memory_space=space)] * len(args),
        out_specs=[pl.BlockSpec(memory_space=pltpu.VMEM)] * len(outs),
        scratch_shapes=[pltpu.VMEM(one, F32) if isinstance(one, tuple) else one for one in scratch],
        compiler_params=pltpu.CompilerParams(vmem_limit_bytes=32 * 1024 * 1024),
    )(*args)


def exchanged(value, axis, by):
    return lax.ppermute(value, axis, [(i, i ^ by) for i in range(lax.axis_size(axis))])


def summed(value, axis):
    count, by = lax.axis_size(axis), 1
    while by < count:
        radix = min(8, count // by)
        terms = [value] + [exchanged(value, axis, k * by) for k in range(1, radix)]
        while len(terms) > 1:
            terms = [a + b for a, b in zip(terms[0::2], terms[1::2])]
        value = terms[0]
        by *= radix
    return value


def carry(consts, own_map):
    count, units = lax.axis_size("tm"), consts.shape[1]
    held = min(WINDOW, count)
    maps = [own_map] + [exchanged(own_map, "tm", k) for k in range(1, held)]
    arrived = []
    for hop in range(count // held - 1):
        (sent,) = call(functools.partial(hop_kernel, held), [consts, *maps, *arrived], [(8, units)])
        arrived = [lax.ppermute(sent, "tm", [(i, (i + held) % count) for i in range(count)])]
    return arrived, maps


def per_device(
    inputs, h_start, in_weight, rec_weight, update_bias, reset_bias, cand_bias, rec_bias
):
    steps, sequences = inputs.shape[0], inputs.shape[1]
    units = rec_weight.shape[0]
    row = lambda value: value.reshape(1, units)
    slots = steps + steps // BLOCK
    rows, wide = (steps, units), (steps, 3 * units)
    fold_outs = [rows, (slots, units, units), (slots, units), (units + 8, units)]
    coefs = [rows] * 5
    gates, prev, mats, vecs, own_map, weight, consts = call(
        first_kernel,
        [inputs.reshape(steps, -1), h_start, in_weight, rec_weight, row(update_bias), row(reset_bias),
         row(cand_bias), row(rec_bias)],
        [wide] + fold_outs + [rec_weight.shape, (8, units)],
        [pltpu.VMEM((steps, in_weight.shape[0]), BF16), pltpu.VMEM(in_weight.shape, BF16), (1, 3 * units),
         (1, units), (1, units), pltpu.SemaphoreType.DMA((8,))] + coefs,
        space=pltpu.HBM,
    )
    sums = []
    for newton in range(ITERS):
        arrived, maps = carry(consts, own_map)
        args = [consts, gates, prev, mats, vecs, weight, *maps, *arrived, *sums]
        kernel = functools.partial(next_kernel, newton, len(maps), len(arrived))
        if newton == ITERS - 1:
            states, total = call(kernel, args, [rows, (8, units)], [rows, (1, units)])
        else:
            total, prev, mats, vecs, own_map = call(
                kernel, args, [(8, units)] + fold_outs, [rows, (1, units)] + coefs
            )
        sums = [total]
    totals = summed(summed(total, "batch"), "tm")[:ITERS, 0]
    denom = lax.axis_size("batch") * sequences * units * (steps * lax.axis_size("tm") + 1) / 2.0
    residual_norms = jnp.sqrt(totals / denom + 1e-06)
    return (states.reshape(steps, sequences, units), residual_norms)


def solution(mesh):
    in_specs = (P("tm", "batch", None), P("batch", None), P(), P(), P(), P(), P(), P())
    out_specs = (P("tm", "batch", None), P())
    return jax.shard_map(
        per_device, mesh=mesh, in_specs=in_specs, out_specs=out_specs, check_vma=False
    )
```

```python
import functools

import jax
import jax.numpy as jnp
from jax import lax
from jax.experimental import pallas as pl
from jax.experimental.pallas import tpu as pltpu
from jax.sharding import PartitionSpec as P

ITERS = 2
BLOCK = 4
WINDOW = 4
PAD = 16
F32 = jnp.float32
BF16 = jnp.bfloat16


def halves(value):
    high = value.astype(BF16)
    return high, (value - high.astype(F32)).astype(BF16)


def paired_rows(value):
    return jnp.concatenate(halves(value), axis=1)


def paired_cols(value):
    both = jnp.concatenate(halves(value), axis=1)
    return jnp.concatenate([both, both], axis=0)


def product(rows, cols):
    width = cols.shape[1]
    both = jnp.dot(paired_rows(rows), paired_cols(cols), preferred_element_type=F32)
    return both[:, :width] + both[:, width:]


def as_column(row):
    units = row.shape[1]
    return jnp.broadcast_to(row, (units, units)).T


def row_times(column, matrix):
    return jnp.sum(column * matrix, axis=0, keepdims=True)


def cell(gates, previous, rec_weight, rec_bias):
    units = previous.shape[1]
    rec = product(previous, rec_weight)
    update = jax.nn.sigmoid(gates[:, :units] + rec[:, :units])
    reset = jax.nn.sigmoid(gates[:, units : 2 * units] + rec[:, units : 2 * units])
    recur = rec[:, 2 * units :] + rec_bias
    cand = jnp.tanh(gates[:, 2 * units :] + reset * recur)
    stepped = (1.0 - update) * cand + update * previous
    return update, reset, recur, cand, stepped


def walk(first, refs, place, stop):
    state = first
    for other in range(stop):
        state = through(state, refs[place ^ other] if len(refs) > 1 else refs[0].at[other])
    return state


def group_start(consts_ref, arrived_refs):
    start = consts_ref[0:1, :]
    if not arrived_refs:
        return start
    return jnp.where(lax.axis_index("tm") < WINDOW, start, arrived_refs[0][0:1, :])


def through(state, one_map):
    units = state.shape[1]
    column = as_column(state - one_map[units + 1 : units + 2, :])
    return row_times(column, one_map[:units, :]) + one_map[units : units + 1, :]


def fold(parts, prev_ref, weight_ref, coef_refs, mats_ref, vecs_ref, map_ref):
    update, reset, recur, cand, stepped = parts
    steps, units = update.shape
    previous = prev_ref[...]
    update_ref, coef_update_ref, coef_reset_ref, coef_cand_ref, step_ref = coef_refs
    common = (1.0 - update) * (1.0 - cand * cand)
    update_ref[...] = update
    coef_update_ref[...] = (previous - cand) * update * (1.0 - update)
    coef_reset_ref[...] = common * recur * reset * (1.0 - reset)
    coef_cand_ref[...] = common * reset
    step_ref[...] = stepped
    row = lax.broadcasted_iota(jnp.int32, (units, units), 0)
    col = lax.broadcasted_iota(jnp.int32, (units, units), 1)

    def slope(t):
        return (
            weight_ref[:, :units] * coef_update_ref[t : t + 1, :]
            + weight_ref[:, units : 2 * units] * coef_reset_ref[t : t + 1, :]
            + weight_ref[:, 2 * units :] * coef_cand_ref[t : t + 1, :]
        )

    def stacked(mat, vec):
        return jnp.concatenate([mat, jnp.broadcast_to(vec, (PAD, units))], axis=0)

    blocks = steps // BLOCK
    for inner in range(BLOCK):
        for block in range(blocks):
            t = block * BLOCK + inner
            keep = update_ref[t : t + 1, :]
            if inner == 0:
                mat = slope(t) + jnp.where(row == col, keep, 0.0)
                vec = step_ref[t : t + 1, :]
            else:
                before = stacked(mats_ref[t - 1], vecs_ref[t - 1 : t, :] - prev_ref[t : t + 1, :])
                after = product(before, slope(t)) + before * keep
                mat = after[:units]
                vec = after[units : units + 1] + step_ref[t : t + 1, :]
            mats_ref[t] = mat
            vecs_ref[t : t + 1, :] = vec

    items = [(b * BLOCK, (b + 1) * BLOCK - 1) for b in range(blocks)]
    free = steps
    while len(items) > 1:
        joined = []
        for (first, early), (second, late) in zip(items[0::2], items[1::2]):
            before = stacked(mats_ref[early], vecs_ref[early : early + 1, :] - prev_ref[second : second + 1, :])
            after = product(before, mats_ref[late])
            mats_ref[free] = after[:units]
            vecs_ref[free : free + 1, :] = after[units : units + 1] + vecs_ref[late : late + 1, :]
            joined.append((first, free))
            free += 1
        items = joined
    last = items[0][1]
    copies = [map_ref] if len(map_ref.shape) == 2 else [map_ref.at[i] for i in range(map_ref.shape[0])]
    for one in copies:
        one[:units, :] = mats_ref[last]
        one[units : units + 1, :] = vecs_ref[last : last + 1, :]
        one[units + 1 : units + 2, :] = prev_ref[0:1, :]
        one[units + 2 :, :] = jnp.zeros((6, units), F32)


def unfold(entering, prev_ref, mats_ref, vecs_ref, out_ref):
    steps = prev_ref.shape[0]
    blocks = steps // BLOCK
    starts = {0: entering}
    slots = {(b, 1): (b + 1) * BLOCK - 1 for b in range(blocks)}
    free, span = steps, 2
    while span <= blocks:
        for b in range(0, blocks, span):
            slots[(b, span)] = free
            free += 1
        span *= 2
    order = sorted(range(blocks), key=lambda b: (bin(b).count("1"), b))
    for b in order:
        t = b * BLOCK
        column = as_column(starts[b] - prev_ref[t : t + 1, :])
        span = 2
        while b % span == 0 and b + span < blocks:
            slot = slots[(b, span)]
            starts[b + span] = row_times(column, mats_ref[slot]) + vecs_ref[slot : slot + 1, :]
            span *= 2
        for inner in range(BLOCK):
            state = row_times(column, mats_ref[t + inner]) + vecs_ref[t + inner : t + inner + 1, :]
            out_ref[t + inner : t + inner + 1, :] = state
        if b % 2 == 0 and b + 1 < blocks:
            starts[b + 1] = state


def shift_in(entering, states_ref, prev_ref):
    steps = states_ref.shape[0]
    prev_ref[0:1, :] = entering
    prev_ref[1:steps, :] = states_ref[0 : steps - 1, :]


def weighted_square(states, stepped):
    steps = states.shape[0]
    mine, count = lax.axis_index("tm"), lax.axis_size("tm")
    position = mine * steps + lax.broadcasted_iota(jnp.int32, states.shape, 0)
    weights = (position.astype(F32) + 1.0) / (steps * count)
    return jnp.sum(weights * (states - stepped) ** 2, axis=(0, 1), keepdims=True)


def first_kernel(
    inputs_hbm, start_hbm, in_weight_hbm, weight_hbm, update_bias_hbm, reset_bias_hbm, cand_bias_hbm,
    rec_bias_hbm,
    gates_ref, prev_ref, mats_ref, vecs_ref, map_ref, weight_ref, consts_ref,
    inputs_ref, in_weight_ref, bias_ref, start_ref, rec_bias_ref, sems, *coef_refs
):
    steps, units = prev_ref.shape
    moves = [
        (inputs_hbm, inputs_ref), (in_weight_hbm, in_weight_ref), (weight_hbm, weight_ref),
        (update_bias_hbm, bias_ref.at[:, pl.ds(0, units)]),
        (reset_bias_hbm, bias_ref.at[:, pl.ds(units, units)]),
        (cand_bias_hbm, bias_ref.at[:, pl.ds(2 * units, units)]),
        (start_hbm, start_ref), (rec_bias_hbm, rec_bias_ref),
    ]
    copies = [pltpu.make_async_copy(src, dst, sems.at[i]) for i, (src, dst) in enumerate(moves)]
    for copy in copies:
        copy.start()
    for copy in copies:
        copy.wait()
    consts_ref[0:1, :] = start_ref[...]
    consts_ref[1:2, :] = rec_bias_ref[...]
    consts_ref[2:, :] = jnp.zeros((6, units), F32)
    gates = jnp.dot(inputs_ref[...], in_weight_ref[...], preferred_element_type=F32) + bias_ref[...]
    gates_ref[...] = gates
    at_start = (lax.axis_index("tm") == 0) & (lax.broadcasted_iota(jnp.int32, (steps, units), 0) == 0)
    previous = jnp.where(at_start, start_ref[...], 0.0)
    prev_ref[...] = previous
    parts = cell(gates, previous, weight_ref[...], rec_bias_ref[...])
    fold(parts, prev_ref, weight_ref, coef_refs, mats_ref, vecs_ref, map_ref)


def hop_kernel(held, pieces, consts_ref, *refs):
    maps, arrived, sent_ref = refs[:pieces], refs[pieces:-1], refs[-1]
    first = group_start(consts_ref, arrived)
    place = lax.rem(lax.axis_index("tm"), held)
    for mine in range(held):

        @pl.when(place == mine)
        def _():
            state = walk(first, maps, mine, held)
            sent_ref[...] = jnp.broadcast_to(state, sent_ref.shape)


def next_kernel(newton, held, pieces, hops, *refs):
    last = newton == ITERS - 1
    consts_ref, gates_ref, old_prev_ref, old_mats_ref, old_vecs_ref, weight_ref = refs[:6]
    maps, refs = refs[6 : 6 + pieces], refs[6 + pieces :]
    arrived, refs = refs[: min(hops, 1)], refs[min(hops, 1) :]
    if newton > 0:
        sums_ref, refs = refs[0], refs[1:]
    if last:
        states_ref, new_sums_ref, prev_ref, enter_ref = refs
    else:
        new_sums_ref, prev_ref, mats_ref, vecs_ref, map_ref, states_ref, enter_ref, *coef_refs = refs
    first = group_start(consts_ref, arrived)
    place = lax.rem(lax.axis_index("tm"), held)
    for mine in range(held):

        @pl.when(place == mine)
        def _():
            enter_ref[...] = walk(first, maps, mine, mine)

    entering = enter_ref[...]
    unfold(entering, old_prev_ref, old_mats_ref, old_vecs_ref, states_ref)
    shift_in(entering, states_ref, prev_ref)
    parts = cell(gates_ref[...], prev_ref[...], weight_ref[...], consts_ref[1:2, :])
    done = weighted_square(states_ref[...], parts[4])
    lane = lax.broadcasted_iota(jnp.int32, (1, prev_ref.shape[1]), 1)
    sums = jnp.where(lane == newton, done, sums_ref[0:1, :] if newton > 0 else 0.0)
    if last:
        new_sums_ref[...] = jnp.broadcast_to(sums[None], new_sums_ref.shape)
    else:
        new_sums_ref[...] = jnp.broadcast_to(sums, new_sums_ref.shape)
    if not last:
        fold(parts, prev_ref, weight_ref, coef_refs, mats_ref, vecs_ref, map_ref)


def call(kernel, args, outs, scratch=(), space=pltpu.VMEM):
    args = [pltpu.with_memory_space_constraint(arg, space) for arg in args]
    return pl.pallas_call(
        kernel,
        out_shape=[jax.ShapeDtypeStruct(shape, F32) for shape in outs],
        in_specs=[pl.BlockSpec(memory_space=space)] * len(args),
        out_specs=[pl.BlockSpec(memory_space=pltpu.VMEM)] * len(outs),
        scratch_shapes=[pltpu.VMEM(one, F32) if isinstance(one, tuple) else one for one in scratch],
        compiler_params=pltpu.CompilerParams(vmem_limit_bytes=32 * 1024 * 1024),
    )(*args)


def exchanged(value, axis, by):
    return lax.ppermute(value, axis, [(i, i ^ by) for i in range(lax.axis_size(axis))])


def carry(consts, own_map, newton):
    count, units = lax.axis_size("tm"), consts.shape[1]
    held = min(WINDOW, count)
    if newton == 0:
        groups = [list(range(first, first + held)) for first in range(0, count, held)]
        maps = [lax.all_to_all(own_map, "tm", 0, 0, axis_index_groups=groups)]
    else:
        maps = [own_map] + [exchanged(own_map, "tm", k) for k in range(1, held)]
    arrived = []
    for hop in range(count // held - 1):
        (sent,) = call(functools.partial(hop_kernel, held, len(maps)), [consts, *maps, *arrived], [(8, units)])
        arrived = [lax.ppermute(sent, "tm", [(i, (i + held) % count) for i in range(count)])]
    return arrived, maps


def per_device(
    inputs, h_start, in_weight, rec_weight, update_bias, reset_bias, cand_bias, rec_bias
):
    steps, sequences = inputs.shape[0], inputs.shape[1]
    units = rec_weight.shape[0]
    row = lambda value: value.reshape(1, units)
    slots = steps + steps // BLOCK
    rows, wide = (steps, units), (steps, 3 * units)
    fold_outs = [rows, (slots, units, units), (slots, units), (units + 8, units)]
    coefs = [rows] * 5
    gates, prev, mats, vecs, own_map, weight, consts = call(
        first_kernel,
        [inputs.reshape(steps, -1), h_start, in_weight, rec_weight, row(update_bias), row(reset_bias),
         row(cand_bias), row(rec_bias)],
        [wide] + fold_outs[:3] + [(min(WINDOW, lax.axis_size("tm")), units + 8, units), rec_weight.shape, (8, units)],
        [pltpu.VMEM((steps, in_weight.shape[0]), BF16), pltpu.VMEM(in_weight.shape, BF16), (1, 3 * units),
         (1, units), (1, units), pltpu.SemaphoreType.DMA((8,))] + coefs,
        space=pltpu.HBM,
    )
    sums = []
    devices = lax.axis_size(("tm", "batch"))
    for newton in range(ITERS):
        arrived, maps = carry(consts, own_map, newton)
        args = [consts, gates, prev, mats, vecs, weight, *maps, *arrived, *sums]
        kernel = functools.partial(next_kernel, newton, min(WINDOW, lax.axis_size('tm')), len(maps), len(arrived))
        if newton == ITERS - 1:
            states, total = call(kernel, args, [rows, (devices, 1, units)], [rows, (1, units)])
        else:
            total, prev, mats, vecs, own_map = call(
                kernel, args, [(8, units)] + fold_outs, [rows, (1, units)] + coefs
            )
        sums = [total]
    totals = jnp.sum(lax.all_to_all(total, ("tm", "batch"), 0, 0, tiled=True), axis=(0, 1))[:ITERS]
    denom = lax.axis_size("batch") * sequences * units * (steps * lax.axis_size("tm") + 1) / 2.0
    residual_norms = jnp.sqrt(totals / denom + 1e-06)
    return (states.reshape(steps, sequences, units), residual_norms)


def solution(mesh):
    in_specs = (P("tm", "batch", None), P("batch", None), P(), P(), P(), P(), P(), P())
    out_specs = (P("tm", "batch", None), P())
    return jax.shard_map(
        per_device, mesh=mesh, in_specs=in_specs, out_specs=out_specs, check_vma=False
    )
```

```python
import functools

import jax
import jax.numpy as jnp
from jax import lax
from jax.experimental import pallas as pl
from jax.experimental.pallas import tpu as pltpu
from jax.sharding import PartitionSpec as P

ITERS = 2
SPAN = 4
CHAINS = 16
PAD = 16
F32 = jnp.float32
BF16 = jnp.bfloat16


def halves(value):
    high = value.astype(BF16)
    return high, (value - high.astype(F32)).astype(BF16)


def paired_rows(value):
    return jnp.concatenate(halves(value), axis=1)


def paired_cols(value):
    both = jnp.concatenate(halves(value), axis=1)
    return jnp.concatenate([both, both], axis=0)


def product(rows, cols):
    width = cols.shape[1]
    both = jnp.dot(paired_rows(rows), paired_cols(cols), preferred_element_type=F32)
    return both[:, :width] + both[:, width:]


def as_column(row):
    units = row.shape[1]
    return jnp.broadcast_to(row, (units, units)).T


def row_times(column, matrix):
    return jnp.sum(column * matrix, axis=0, keepdims=True)


def cell(gates, previous, rec_weight, rec_bias):
    units = previous.shape[1]
    rec = product(previous, rec_weight)
    update = jax.nn.sigmoid(gates[:, :units] + rec[:, :units])
    reset = jax.nn.sigmoid(gates[:, units : 2 * units] + rec[:, units : 2 * units])
    recur = rec[:, 2 * units :] + rec_bias
    cand = jnp.tanh(gates[:, 2 * units :] + reset * recur)
    stepped = (1.0 - update) * cand + update * previous
    return update, reset, recur, cand, stepped


def group_start(consts_ref, arrived_refs):
    start = consts_ref[0:1, :]
    if not arrived_refs:
        return start
    return jnp.where(lax.axis_index("tm") < SPAN, start, arrived_refs[0][0:1, :])


def through(state, one_map):
    units = state.shape[1]
    column = as_column(state - one_map[units + 1 : units + 2, :])
    return row_times(column, one_map[:units, :]) + one_map[units : units + 1, :]


def joins(steps):
    size = steps // CHAINS
    slots = {(b, 1): (b + 1) * size - 1 for b in range(CHAINS)}
    free, span = steps, 2
    while span <= CHAINS:
        for b in range(0, CHAINS, span):
            slots[(b, span)] = free
            free += 1
        span *= 2
    return slots


def fold(parts, prev_ref, weight_ref, coef_refs, mats_ref, vecs_ref, map_ref):
    update, reset, recur, cand, stepped = parts
    steps, units = update.shape
    size = steps // CHAINS
    previous = prev_ref[...]
    update_ref, coef_update_ref, coef_reset_ref, coef_cand_ref, step_ref = coef_refs
    common = (1.0 - update) * (1.0 - cand * cand)
    update_ref[...] = update
    coef_update_ref[...] = (previous - cand) * update * (1.0 - update)
    coef_reset_ref[...] = common * recur * reset * (1.0 - reset)
    coef_cand_ref[...] = common * reset
    step_ref[...] = stepped
    row = lax.broadcasted_iota(jnp.int32, (units, units), 0)
    col = lax.broadcasted_iota(jnp.int32, (units, units), 1)

    def slope(t):
        return (
            weight_ref[:, :units] * coef_update_ref[pl.ds(t, 1), :]
            + weight_ref[:, units : 2 * units] * coef_reset_ref[pl.ds(t, 1), :]
            + weight_ref[:, 2 * units :] * coef_cand_ref[pl.ds(t, 1), :]
        )

    def stacked(mat, vec):
        return jnp.concatenate([mat, jnp.broadcast_to(vec, (PAD, units))], axis=0)

    for block in range(CHAINS):
        t = block * size
        mats_ref[t] = slope(t) + jnp.where(row == col, update_ref[t : t + 1, :], 0.0)
        vecs_ref[t : t + 1, :] = step_ref[t : t + 1, :]

    def advance(inner, carried):
        for block in range(CHAINS):
            t = block * size + inner
            shifted = vecs_ref[pl.ds(t - 1, 1), :] - prev_ref[pl.ds(t, 1), :]
            before = stacked(mats_ref[t - 1], shifted)
            after = product(before, slope(t)) + before * update_ref[pl.ds(t, 1), :]
            mats_ref[t] = after[:units]
            vecs_ref[pl.ds(t, 1), :] = after[units : units + 1] + step_ref[pl.ds(t, 1), :]
        return carried

    lax.fori_loop(1, size, advance, 0)

    slots = joins(steps)
    for (first, span), slot in slots.items():
        if span > 1:
            second = first + span // 2
            early, late = slots[(first, span // 2)], slots[(second, span // 2)]
            shifted = vecs_ref[early : early + 1, :] - prev_ref[second * size : second * size + 1, :]
            after = product(stacked(mats_ref[early], shifted), mats_ref[late])
            mats_ref[slot] = after[:units]
            vecs_ref[slot : slot + 1, :] = after[units : units + 1] + vecs_ref[late : late + 1, :]
    last = slots[(0, CHAINS)]
    map_ref[:units, :] = mats_ref[last]
    map_ref[units : units + 1, :] = vecs_ref[last : last + 1, :]
    map_ref[units + 1 : units + 2, :] = prev_ref[0:1, :]
    map_ref[units + 2 :, :] = jnp.zeros((6, units), F32)


def unfold(entering, prev_ref, mats_ref, vecs_ref, out_ref):
    steps = prev_ref.shape[0]
    size = steps // CHAINS
    slots = joins(steps)
    starts = {0: entering}
    for b in sorted(range(CHAINS), key=lambda b: (bin(b).count("1"), -b)):
        t = b * size
        column = as_column(starts[b] - prev_ref[t : t + 1, :])
        span = 1
        while b % (2 * span) == 0 and b + span < CHAINS:
            slot = slots[(b, span)]
            starts[b + span] = row_times(column, mats_ref[slot]) + vecs_ref[slot : slot + 1, :]
            span *= 2
        for inner in range(size):
            state = row_times(column, mats_ref[t + inner]) + vecs_ref[t + inner : t + inner + 1, :]
            out_ref[t + inner : t + inner + 1, :] = state


def shift_in(entering, states_ref, prev_ref):
    steps = states_ref.shape[0]
    prev_ref[0:1, :] = entering
    prev_ref[1:steps, :] = states_ref[0 : steps - 1, :]


def weighted_square(states, stepped):
    steps = states.shape[0]
    group, count = lax.axis_index("tm") // SPAN, lax.axis_size("tm") // SPAN
    position = group * steps + lax.broadcasted_iota(jnp.int32, states.shape, 0)
    weights = (position.astype(F32) + 1.0) / (steps * count)
    return jnp.sum(weights * (states - stepped) ** 2, axis=(0, 1), keepdims=True)


def send_on(start, map_ref, sent_ref):
    sent_ref[...] = jnp.broadcast_to(through(start, map_ref), sent_ref.shape)


def fetch_kernel(
    inputs_hbm, start_hbm, in_weight_hbm, weight_hbm, update_bias_hbm, reset_bias_hbm, cand_bias_hbm,
    rec_bias_hbm,
    wide_ref, in_weight_ref, weight_ref, bias_ref, consts_ref,
    inputs_ref, start_ref, rec_bias_ref, sems
):
    units = weight_ref.shape[0]
    moves = [
        (inputs_hbm, inputs_ref), (in_weight_hbm, in_weight_ref), (weight_hbm, weight_ref),
        (update_bias_hbm, bias_ref.at[:, pl.ds(0, units)]),
        (reset_bias_hbm, bias_ref.at[:, pl.ds(units, units)]),
        (cand_bias_hbm, bias_ref.at[:, pl.ds(2 * units, units)]),
        (start_hbm, start_ref), (rec_bias_hbm, rec_bias_ref),
    ]
    copies = [pltpu.make_async_copy(src, dst, sems.at[i]) for i, (src, dst) in enumerate(moves)]
    for copy in copies:
        copy.start()
    for copy in copies:
        copy.wait()
    wide_ref[...] = inputs_ref[...].astype(F32)
    consts_ref[0:1, :] = start_ref[...]
    consts_ref[1:2, :] = rec_bias_ref[...]
    consts_ref[2:, :] = jnp.zeros((6, units), F32)


def first_kernel(consts_ref, in_weight_ref, bias_ref, weight_ref, *refs):
    shares, refs = refs[:SPAN], refs[SPAN:]
    gates_ref, prev_ref, mats_ref, vecs_ref, map_ref, sent_ref, held_ref, *coef_refs = refs
    steps, units = prev_ref.shape
    mine = lax.axis_index("tm")
    place = lax.rem(mine, SPAN)
    for k in range(SPAN):
        held_ref[k] = shares[k][...]
    inputs = jnp.concatenate([held_ref[place ^ j] for j in range(SPAN)], axis=0).astype(BF16)
    gates = jnp.dot(inputs, in_weight_ref[...], preferred_element_type=F32) + bias_ref[...]
    gates_ref[...] = gates
    start = consts_ref[0:1, :]
    at_start = (mine < SPAN) & (lax.broadcasted_iota(jnp.int32, (steps, units), 0) == 0)
    previous = jnp.where(at_start, start, 0.0)
    prev_ref[...] = previous
    parts = cell(gates, previous, weight_ref[...], consts_ref[1:2, :])
    fold(parts, prev_ref, weight_ref, coef_refs, mats_ref, vecs_ref, map_ref)
    send_on(start, map_ref, sent_ref)


def hop_kernel(consts_ref, map_ref, arrived_ref, sent_ref):
    send_on(group_start(consts_ref, [arrived_ref]), map_ref, sent_ref)


def next_kernel(newton, hops, *refs):
    last = newton == ITERS - 1
    consts_ref, gates_ref, old_prev_ref, old_mats_ref, old_vecs_ref, weight_ref = refs[:6]
    arrived, refs = refs[6 : 6 + hops], refs[6 + hops :]
    if newton > 0:
        sums_ref, refs = refs[0], refs[1:]
    if last:
        out_ref, new_sums_ref, prev_ref, states_ref = refs
    else:
        new_sums_ref, prev_ref, mats_ref, vecs_ref, map_ref, sent_ref, states_ref, *coef_refs = refs
    entering = group_start(consts_ref, arrived)
    unfold(entering, old_prev_ref, old_mats_ref, old_vecs_ref, states_ref)
    shift_in(entering, states_ref, prev_ref)
    if last:
        share = out_ref.shape[0]
        first = pl.multiple_of(lax.rem(lax.axis_index("tm"), SPAN) * share, share)
        out_ref[...] = states_ref[pl.ds(first, share), :]
    parts = cell(gates_ref[...], prev_ref[...], weight_ref[...], consts_ref[1:2, :])
    done = weighted_square(states_ref[...], parts[4])
    lane = lax.broadcasted_iota(jnp.int32, new_sums_ref.shape, 1)
    new_sums_ref[...] = jnp.where(lane == newton, done, sums_ref[...] if newton > 0 else 0.0)
    if not last:
        fold(parts, prev_ref, weight_ref, coef_refs, mats_ref, vecs_ref, map_ref)
        send_on(consts_ref[0:1, :], map_ref, sent_ref)


def call(kernel, args, outs, scratch=(), space=pltpu.VMEM):
    args = [pltpu.with_memory_space_constraint(arg, space) for arg in args]
    return pl.pallas_call(
        kernel,
        out_shape=[jax.ShapeDtypeStruct(o, F32) if isinstance(o, tuple) else o for o in outs],
        in_specs=[pl.BlockSpec(memory_space=space)] * len(args),
        out_specs=[pl.BlockSpec(memory_space=pltpu.VMEM)] * len(outs),
        scratch_shapes=[pltpu.VMEM(one, F32) if isinstance(one, tuple) else one for one in scratch],
        compiler_params=pltpu.CompilerParams(vmem_limit_bytes=24 * 1024 * 1024),
    )(*args)


def exchanged(value, axis, by):
    return lax.ppermute(value, axis, [(i, i ^ by) for i in range(lax.axis_size(axis))])


def summed(value, axis, by=1):
    count = lax.axis_size(axis)
    while by < count:
        radix = min(4, count // by)
        terms = [value] + [exchanged(value, axis, k * by) for k in range(1, radix)]
        while len(terms) > 1:
            terms = [a + b for a, b in zip(terms[0::2], terms[1::2])]
        value = terms[0]
        by *= radix
    return value


def carry(consts, own_map, sent):
    count = lax.axis_size("tm")
    ring = [(i, (i + SPAN) % count) for i in range(count)]
    arrived = []
    for hop in range(count // SPAN - 1):
        if hop > 0:
            (sent,) = call(hop_kernel, [consts, own_map, *arrived], [sent.shape])
        arrived = [lax.ppermute(sent, "tm", ring)]
    return arrived


def per_device(
    inputs, h_start, in_weight, rec_weight, update_bias, reset_bias, cand_bias, rec_bias
):
    share, sequences = inputs.shape[0], inputs.shape[1]
    units = rec_weight.shape[0]
    row = lambda value: value.reshape(1, units)
    steps = share * SPAN
    slots = steps + CHAINS
    rows, wide = (steps, units), (steps, 3 * units)
    fold_outs = [rows, (slots, units, units), (slots, units), (units + 8, units), (8, units)]
    coefs = [rows] * 5
    own, in_rows, weight, bias, consts = call(
        fetch_kernel,
        [inputs.reshape(share, -1), h_start, in_weight, rec_weight, row(update_bias), row(reset_bias),
         row(cand_bias), row(rec_bias)],
        [(share, units), jax.ShapeDtypeStruct(in_weight.shape, BF16), rec_weight.shape, (1, 3 * units),
         (8, units)],
        [pltpu.VMEM((share, units), BF16), (1, units), (1, units), pltpu.SemaphoreType.DMA((8,))],
        space=pltpu.HBM,
    )
    shares = [own] + [exchanged(own, "tm", k) for k in range(1, SPAN)]
    gates, prev, mats, vecs, own_map, sent = call(
        first_kernel, [consts, in_rows, bias, weight, *shares], [wide] + fold_outs,
        [(SPAN, share, units)] + coefs,
    )
    sums = []
    for newton in range(ITERS):
        arrived = carry(consts, own_map, sent)
        args = [consts, gates, prev, mats, vecs, weight, *arrived, *sums]
        kernel = functools.partial(next_kernel, newton, len(arrived))
        if newton == ITERS - 1:
            states, total = call(kernel, args, [(share, units), (8, units)], [rows, rows])
        else:
            total, prev, mats, vecs, own_map, sent = call(
                kernel, args, [(8, units)] + fold_outs, [rows] + coefs
            )
        sums = [total]
    totals = summed(summed(total, "batch"), "tm", SPAN)[0, :ITERS]
    denom = lax.axis_size("batch") * sequences * units * (share * lax.axis_size("tm") + 1) / 2.0
    residual_norms = jnp.sqrt(totals / denom + 1e-06)
    return (states.reshape(share, sequences, units), residual_norms)


def solution(mesh):
    in_specs = (P("tm", "batch", None), P("batch", None), P(), P(), P(), P(), P(), P())
    out_specs = (P("tm", "batch", None), P())
    return jax.shard_map(
        per_device, mesh=mesh, in_specs=in_specs, out_specs=out_specs, check_vma=False
    )
```

```python
import functools

import jax
import jax.numpy as jnp
from jax import lax
from jax.experimental import pallas as pl
from jax.experimental.pallas import tpu as pltpu
from jax.sharding import PartitionSpec as P

ITERS = 2
SPAN = 4
CHAINS = 16
PAD = 16
F32 = jnp.float32
BF16 = jnp.bfloat16


def halves(value):
    high = value.astype(BF16)
    return high, (value - high.astype(F32)).astype(BF16)


def paired_rows(value):
    return jnp.concatenate(halves(value), axis=1)


def paired_cols(value):
    both = jnp.concatenate(halves(value), axis=1)
    return jnp.concatenate([both, both], axis=0)


def product(rows, cols):
    width = cols.shape[1]
    both = jnp.dot(paired_rows(rows), paired_cols(cols), preferred_element_type=F32)
    return both[:, :width] + both[:, width:]


def as_column(row):
    units = row.shape[1]
    return jnp.broadcast_to(row, (units, units)).T


def row_times(column, matrix):
    return jnp.sum(column * matrix, axis=0, keepdims=True)


def cell(gates, previous, rec_weight, rec_bias):
    units = previous.shape[1]
    rec = product(previous, rec_weight)
    update = jax.nn.sigmoid(gates[:, :units] + rec[:, :units])
    reset = jax.nn.sigmoid(gates[:, units : 2 * units] + rec[:, units : 2 * units])
    recur = rec[:, 2 * units :] + rec_bias
    cand = jnp.tanh(gates[:, 2 * units :] + reset * recur)
    stepped = (1.0 - update) * cand + update * previous
    return update, reset, recur, cand, stepped


def group():
    return lax.axis_index("tm") // SPAN


def through(state, one_map):
    units = state.shape[1]
    column = as_column(state - one_map[units + 1 : units + 2, :])
    return row_times(column, one_map[:units, :]) + one_map[units : units + 1, :]


def joins(steps):
    size = steps // CHAINS
    slots = {(b, 1): (b + 1) * size - 1 for b in range(CHAINS)}
    free, span = steps, 2
    while span <= CHAINS:
        for b in range(0, CHAINS, span):
            slots[(b, span)] = free
            free += 1
        span *= 2
    return slots


def fold(parts, prev_ref, weight_ref, coef_refs, mats_ref, vecs_ref, map_ref):
    update, reset, recur, cand, stepped = parts
    steps, units = update.shape
    size = steps // CHAINS
    previous = prev_ref[...]
    update_ref, coef_update_ref, coef_reset_ref, coef_cand_ref, step_ref = coef_refs
    common = (1.0 - update) * (1.0 - cand * cand)
    update_ref[...] = update
    coef_update_ref[...] = (previous - cand) * update * (1.0 - update)
    coef_reset_ref[...] = common * recur * reset * (1.0 - reset)
    coef_cand_ref[...] = common * reset
    step_ref[...] = stepped
    row = lax.broadcasted_iota(jnp.int32, (units, units), 0)
    col = lax.broadcasted_iota(jnp.int32, (units, units), 1)

    def slope(t):
        return (
            weight_ref[:, :units] * coef_update_ref[t : t + 1, :]
            + weight_ref[:, units : 2 * units] * coef_reset_ref[t : t + 1, :]
            + weight_ref[:, 2 * units :] * coef_cand_ref[t : t + 1, :]
        )

    def stacked(mat, vec):
        return jnp.concatenate([mat, jnp.broadcast_to(vec, (PAD, units))], axis=0)

    for block in range(CHAINS):
        t = block * size
        mats_ref[t] = slope(t) + jnp.where(row == col, update_ref[t : t + 1, :], 0.0)
        vecs_ref[t : t + 1, :] = step_ref[t : t + 1, :]

    for inner in range(1, size):
        for block in range(CHAINS):
            t = block * size + inner
            before = stacked(mats_ref[t - 1], vecs_ref[t - 1 : t, :] - prev_ref[t : t + 1, :])
            after = product(before, slope(t)) + before * update_ref[t : t + 1, :]
            mats_ref[t] = after[:units]
            vecs_ref[t : t + 1, :] = after[units : units + 1] + step_ref[t : t + 1, :]

    slots = joins(steps)
    for (first, span), slot in slots.items():
        if span > 1:
            second = first + span // 2
            early, late = slots[(first, span // 2)], slots[(second, span // 2)]
            shifted = vecs_ref[early : early + 1, :] - prev_ref[second * size : second * size + 1, :]
            after = product(stacked(mats_ref[early], shifted), mats_ref[late])
            mats_ref[slot] = after[:units]
            vecs_ref[slot : slot + 1, :] = after[units : units + 1] + vecs_ref[late : late + 1, :]
    last = slots[(0, CHAINS)]
    map_ref[:units, :] = mats_ref[last]
    map_ref[units : units + 1, :] = vecs_ref[last : last + 1, :]
    map_ref[units + 1 : units + 2, :] = prev_ref[0:1, :]
    map_ref[units + 2 :, :] = jnp.zeros((6, units), F32)


def unfold(entering, prev_ref, mats_ref, vecs_ref, out_ref):
    steps = prev_ref.shape[0]
    size = steps // CHAINS
    slots = joins(steps)
    starts = {0: entering}
    for b in sorted(range(CHAINS), key=lambda b: (bin(b).count("1"), -b)):
        t = b * size
        column = as_column(starts[b] - prev_ref[t : t + 1, :])
        span = 1
        while b % (2 * span) == 0 and b + span < CHAINS:
            slot = slots[(b, span)]
            starts[b + span] = row_times(column, mats_ref[slot]) + vecs_ref[slot : slot + 1, :]
            span *= 2
        for inner in range(size):
            state = row_times(column, mats_ref[t + inner]) + vecs_ref[t + inner : t + inner + 1, :]
            out_ref[t + inner : t + inner + 1, :] = state


def shift_in(entering, states_ref, prev_ref):
    steps = states_ref.shape[0]
    prev_ref[0:1, :] = entering
    prev_ref[1:steps, :] = states_ref[0 : steps - 1, :]


def weighted_square(states, stepped):
    steps = states.shape[0]
    count = lax.axis_size("tm") // SPAN
    position = group() * steps + lax.broadcasted_iota(jnp.int32, states.shape, 0)
    weights = (position.astype(F32) + 1.0) / (steps * count)
    return jnp.sum(weights * (states - stepped) ** 2, axis=(0, 1), keepdims=True)


def send_on(start, map_ref, sent_ref):
    sent_ref[...] = jnp.broadcast_to(through(start, map_ref), sent_ref.shape)


def fetch_kernel(
    inputs_hbm, start_hbm, in_weight_hbm, weight_hbm, update_bias_hbm, reset_bias_hbm, cand_bias_hbm,
    rec_bias_hbm,
    wide_ref, in_weight_ref, weight_ref, bias_ref, consts_ref,
    inputs_ref, start_ref, rec_bias_ref, sems
):
    units = weight_ref.shape[0]
    moves = [
        (inputs_hbm, inputs_ref), (in_weight_hbm, in_weight_ref), (weight_hbm, weight_ref),
        (update_bias_hbm, bias_ref.at[:, pl.ds(0, units)]),
        (reset_bias_hbm, bias_ref.at[:, pl.ds(units, units)]),
        (cand_bias_hbm, bias_ref.at[:, pl.ds(2 * units, units)]),
        (start_hbm, start_ref), (rec_bias_hbm, rec_bias_ref),
    ]
    copies = [pltpu.make_async_copy(src, dst, sems.at[i]) for i, (src, dst) in enumerate(moves)]
    for copy in copies:
        copy.start()
    for copy in copies:
        copy.wait()
    wide_ref[...] = inputs_ref[...].astype(F32)
    consts_ref[0:1, :] = start_ref[...]
    consts_ref[1:2, :] = rec_bias_ref[...]
    consts_ref[2:, :] = jnp.zeros((6, units), F32)


def first_kernel(consts_ref, in_weight_ref, bias_ref, weight_ref, *refs):
    shares, refs = refs[:SPAN], refs[SPAN:]
    gates_ref, sums_ref, prev_ref, mats_ref, vecs_ref, sent_ref, map_ref, held_ref, *coef_refs = refs
    sums_ref[...] = jnp.zeros(sums_ref.shape, F32)
    steps, units = prev_ref.shape
    mine = lax.axis_index("tm")
    place = lax.rem(mine, SPAN)
    for k in range(SPAN):
        held_ref[k] = shares[k][...]
    inputs = jnp.concatenate([held_ref[place ^ j] for j in range(SPAN)], axis=0).astype(BF16)
    gates = jnp.dot(inputs, in_weight_ref[...], preferred_element_type=F32) + bias_ref[...]
    gates_ref[...] = gates
    start = consts_ref[0:1, :]
    at_start = (mine < SPAN) & (lax.broadcasted_iota(jnp.int32, (steps, units), 0) == 0)
    previous = jnp.where(at_start, start, 0.0)
    prev_ref[...] = previous
    parts = cell(gates, previous, weight_ref[...], consts_ref[1:2, :])
    fold(parts, prev_ref, weight_ref, coef_refs, mats_ref, vecs_ref, map_ref)
    send_on(start, map_ref, sent_ref)


def hop_kernel(sent_first_ref, map_ref, arrived_ref, sent_ref):
    state = through(arrived_ref[0:1, :], map_ref)
    sent_ref[...] = jnp.where(group() == 0, sent_first_ref[...], state)


def middle_kernel(
    newton, at_front, start_ref, consts_ref, gates_ref, weight_ref, old_prev_ref, old_mats_ref, old_vecs_ref,
    sums_ref, new_sums_ref, new_prev_ref, mats_ref, vecs_ref, sent_ref, map_ref, states_ref, *coef_refs
):
    @pl.when((group() == 0) == at_front)
    def _():
        entering = start_ref[0:1, :]
        unfold(entering, old_prev_ref, old_mats_ref, old_vecs_ref, states_ref)
        shift_in(entering, states_ref, new_prev_ref)
        parts = cell(gates_ref[...], new_prev_ref[...], weight_ref[...], consts_ref[1:2, :])
        add_sum(newton, sums_ref, states_ref, parts, new_sums_ref)
        fold(parts, new_prev_ref, weight_ref, coef_refs, mats_ref, vecs_ref, map_ref)
        send_on(consts_ref[0:1, :], map_ref, sent_ref)


def add_sum(newton, sums_ref, states_ref, parts, new_sums_ref):
    done = weighted_square(states_ref[...], parts[4])
    lane = lax.broadcasted_iota(jnp.int32, new_sums_ref.shape, 1)
    new_sums_ref[...] = jnp.where(lane == newton, done, sums_ref[...])


def last_kernel(newton, sides, consts_ref, gates_ref, weight_ref, *refs):
    sides_refs, refs = [refs[5 * i : 5 * i + 5] for i in range(sides)], refs[5 * sides :]
    out_ref, new_sums_ref, prev_ref, states_ref, sums_ref = refs
    for side, (start_ref, old_prev_ref, old_mats_ref, old_vecs_ref, old_sums_ref) in enumerate(sides_refs):

        @pl.when((group() == 0) == (side == 0))
        def _():
            entering = start_ref[0:1, :]
            unfold(entering, old_prev_ref, old_mats_ref, old_vecs_ref, states_ref)
            shift_in(entering, states_ref, prev_ref)
            sums_ref[...] = old_sums_ref[...]

    share = out_ref.shape[0]
    first = pl.multiple_of(lax.rem(lax.axis_index("tm"), SPAN) * share, share)
    out_ref[...] = states_ref[pl.ds(first, share), :]
    parts = cell(gates_ref[...], prev_ref[...], weight_ref[...], consts_ref[1:2, :])
    add_sum(newton, sums_ref, states_ref, parts, new_sums_ref)


def call(kernel, args, outs, scratch=(), space=pltpu.VMEM):
    args = [pltpu.with_memory_space_constraint(arg, space) for arg in args]
    return pl.pallas_call(
        kernel,
        out_shape=[jax.ShapeDtypeStruct(o, F32) if isinstance(o, tuple) else o for o in outs],
        in_specs=[pl.BlockSpec(memory_space=space)] * len(args),
        out_specs=[pl.BlockSpec(memory_space=pltpu.VMEM)] * len(outs),
        scratch_shapes=[pltpu.VMEM(one, F32) if isinstance(one, tuple) else one for one in scratch],
        compiler_params=pltpu.CompilerParams(vmem_limit_bytes=16 * 1024 * 1024),
    )(*args)


def exchanged(value, axis, by):
    return lax.ppermute(value, axis, [(i, i ^ by) for i in range(lax.axis_size(axis))])


def summed(value, axis, by=1):
    count = lax.axis_size(axis)
    while by < count:
        radix = min(4, count // by)
        terms = [value] + [exchanged(value, axis, k * by) for k in range(1, radix)]
        while len(terms) > 1:
            terms = [a + b for a, b in zip(terms[0::2], terms[1::2])]
        value = terms[0]
        by *= radix
    return value


def carry(sent, own_map):
    count = lax.axis_size("tm")
    onward = [(i, i + SPAN) for i in range(count - SPAN)]
    arrived = lax.ppermute(sent, "tm", onward)
    for _ in range(count // SPAN - 2):
        (further,) = call(hop_kernel, [sent, *own_map, arrived], [sent.shape])
        arrived = lax.ppermute(further, "tm", onward)
    return arrived


def per_device(
    inputs, h_start, in_weight, rec_weight, update_bias, reset_bias, cand_bias, rec_bias
):
    share, sequences = inputs.shape[0], inputs.shape[1]
    units = rec_weight.shape[0]
    row = lambda value: value.reshape(1, units)
    steps = share * SPAN
    slots = steps + CHAINS
    rows, wide = (steps, units), (steps, 3 * units)
    sides = min(2, lax.axis_size("tm") // SPAN)
    fold_outs = [(8, units), rows, (slots, units, units), (slots, units), (8, units)]
    coefs = [rows] * 5
    onward = lax.axis_size("tm") // SPAN > 2
    map_out, map_scratch = [(units + 8, units)] * onward, [(units + 8, units)] * (not onward)
    own, in_rows, weight, bias, consts = call(
        fetch_kernel,
        [inputs.reshape(share, -1), h_start, in_weight, rec_weight, row(update_bias), row(reset_bias),
         row(cand_bias), row(rec_bias)],
        [(share, units), jax.ShapeDtypeStruct(in_weight.shape, BF16), rec_weight.shape, (1, 3 * units),
         (8, units)],
        [pltpu.VMEM((share, units), BF16), (1, units), (1, units), pltpu.SemaphoreType.DMA((8,))],
        space=pltpu.HBM,
    )
    shares = [own] + [exchanged(own, "tm", k) for k in range(1, SPAN)]
    gates, *solved = call(
        first_kernel, [consts, in_rows, bias, weight, *shares], [wide] + fold_outs + map_out,
        map_scratch + [(SPAN, share, units)] + coefs,
    )
    held = [solved] * sides
    for newton in range(ITERS):
        starts = [consts] + [carry(held[0][4], held[-1][5:])] * (sides - 1)
        if newton < ITERS - 1:
            held = [
                call(
                    functools.partial(middle_kernel, newton, side == 0),
                    [starts[side], consts, gates, weight, *held[side][1:4], held[side][0]],
                    fold_outs + map_out,
                    map_scratch + [rows] + coefs,
                )
                for side in range(sides)
            ]
        else:
            args = [one for side in range(sides) for one in (starts[side], *held[side][1:4], held[side][0])]
            states, total = call(
                functools.partial(last_kernel, newton, sides), [consts, gates, weight, *args],
                [(share, units), (8, units)], [rows, rows, (8, units)],
            )
    totals = summed(summed(total, "batch"), "tm", SPAN)[0, :ITERS]
    denom = lax.axis_size("batch") * sequences * units * (share * lax.axis_size("tm") + 1) / 2.0
    residual_norms = jnp.sqrt(totals / denom + 1e-06)
    return (states.reshape(share, sequences, units), residual_norms)


def solution(mesh):
    in_specs = (P("tm", "batch", None), P("batch", None), P(), P(), P(), P(), P(), P())
    out_specs = (P("tm", "batch", None), P())
    return jax.shard_map(
        per_device, mesh=mesh, in_specs=in_specs, out_specs=out_specs, check_vma=False
    )
```

```python
import functools

import jax
import jax.numpy as jnp
from jax import lax
from jax.experimental import pallas as pl
from jax.experimental.pallas import tpu as pltpu
from jax.sharding import PartitionSpec as P

ITERS = 2
SPAN = 4
CHAINS = 16
PAD = 16
F32 = jnp.float32
BF16 = jnp.bfloat16


def halves(value):
    high = value.astype(BF16)
    return high, (value - high.astype(F32)).astype(BF16)


def paired_rows(value):
    return jnp.concatenate(halves(value), axis=1)


def paired_cols(value):
    both = jnp.concatenate(halves(value), axis=1)
    return jnp.concatenate([both, both], axis=0)


def product(rows, cols):
    width = cols.shape[1]
    both = jnp.dot(paired_rows(rows), paired_cols(cols), preferred_element_type=F32)
    return both[:, :width] + both[:, width:]


def as_column(row):
    units = row.shape[1]
    return jnp.broadcast_to(row, (units, units)).T


def row_times(column, matrix):
    return jnp.sum(column * matrix, axis=0, keepdims=True)


def cell(gates, previous, rec_weight, rec_bias):
    units = previous.shape[1]
    rec = product(previous, rec_weight)
    update = jax.nn.sigmoid(gates[:, :units] + rec[:, :units])
    reset = jax.nn.sigmoid(gates[:, units : 2 * units] + rec[:, units : 2 * units])
    recur = rec[:, 2 * units :] + rec_bias
    cand = jnp.tanh(gates[:, 2 * units :] + reset * recur)
    stepped = (1.0 - update) * cand + update * previous
    return update, reset, recur, cand, stepped


def group():
    return lax.axis_index("tm") // SPAN


def through(state, one_map):
    units = state.shape[1]
    column = as_column(state - one_map[units + 1 : units + 2, :])
    return row_times(column, one_map[:units, :]) + one_map[units : units + 1, :]


def joins(steps):
    size = steps // CHAINS
    slots = {(b, 1): (b + 1) * size - 1 for b in range(CHAINS)}
    free, span = steps, 2
    while span <= CHAINS:
        for b in range(0, CHAINS, span):
            slots[(b, span)] = free
            free += 1
        span *= 2
    return slots


def fold(parts, prev_ref, weight_ref, coef_refs, mats_ref, vecs_ref, map_ref):
    update, reset, recur, cand, stepped = parts
    steps, units = update.shape
    size = steps // CHAINS
    previous = prev_ref[...]
    update_ref, coef_update_ref, coef_reset_ref, coef_cand_ref, step_ref = coef_refs
    common = (1.0 - update) * (1.0 - cand * cand)
    update_ref[...] = update
    coef_update_ref[...] = (previous - cand) * update * (1.0 - update)
    coef_reset_ref[...] = common * recur * reset * (1.0 - reset)
    coef_cand_ref[...] = common * reset
    step_ref[...] = stepped
    row = lax.broadcasted_iota(jnp.int32, (units, units), 0)
    col = lax.broadcasted_iota(jnp.int32, (units, units), 1)

    def slope(t):
        return (
            weight_ref[:, :units] * coef_update_ref[t : t + 1, :]
            + weight_ref[:, units : 2 * units] * coef_reset_ref[t : t + 1, :]
            + weight_ref[:, 2 * units :] * coef_cand_ref[t : t + 1, :]
        )

    def stacked(mat, vec):
        return jnp.concatenate([mat, jnp.broadcast_to(vec, (PAD, units))], axis=0)

    for block in range(CHAINS):
        t = block * size
        mats_ref[t] = slope(t) + jnp.where(row == col, update_ref[t : t + 1, :], 0.0)
        vecs_ref[t : t + 1, :] = step_ref[t : t + 1, :]

    for inner in range(1, size):
        for block in range(CHAINS):
            t = block * size + inner
            before = stacked(mats_ref[t - 1], vecs_ref[t - 1 : t, :] - prev_ref[t : t + 1, :])
            after = product(before, slope(t)) + before * update_ref[t : t + 1, :]
            mats_ref[t] = after[:units]
            vecs_ref[t : t + 1, :] = after[units : units + 1] + step_ref[t : t + 1, :]

    slots = joins(steps)
    for (first, span), slot in slots.items():
        if span > 1:
            second = first + span // 2
            early, late = slots[(first, span // 2)], slots[(second, span // 2)]
            shifted = vecs_ref[early : early + 1, :] - prev_ref[second * size : second * size + 1, :]
            after = product(stacked(mats_ref[early], shifted), mats_ref[late])
            mats_ref[slot] = after[:units]
            vecs_ref[slot : slot + 1, :] = after[units : units + 1] + vecs_ref[late : late + 1, :]
    last = slots[(0, CHAINS)]
    map_ref[:units, :] = mats_ref[last]
    map_ref[units : units + 1, :] = vecs_ref[last : last + 1, :]
    map_ref[units + 1 : units + 2, :] = prev_ref[0:1, :]
    map_ref[units + 2 :, :] = jnp.zeros((6, units), F32)


def unfold(entering, prev_ref, mats_ref, vecs_ref, out_ref):
    steps = prev_ref.shape[0]
    size = steps // CHAINS
    slots = joins(steps)
    starts = {0: entering}
    for b in sorted(range(CHAINS), key=lambda b: (bin(b).count("1"), -b)):
        t = b * size
        column = as_column(starts[b] - prev_ref[t : t + 1, :])
        span = 1
        while b % (2 * span) == 0 and b + span < CHAINS:
            slot = slots[(b, span)]
            starts[b + span] = row_times(column, mats_ref[slot]) + vecs_ref[slot : slot + 1, :]
            span *= 2
        for inner in range(size):
            state = row_times(column, mats_ref[t + inner]) + vecs_ref[t + inner : t + inner + 1, :]
            out_ref[t + inner : t + inner + 1, :] = state


def shift_in(entering, states_ref, prev_ref):
    steps = states_ref.shape[0]
    prev_ref[0:1, :] = entering
    prev_ref[1:steps, :] = states_ref[0 : steps - 1, :]


def weighted_square(states, stepped):
    steps = states.shape[0]
    count = lax.axis_size("tm") // SPAN
    position = group() * steps + lax.broadcasted_iota(jnp.int32, states.shape, 0)
    weights = (position.astype(F32) + 1.0) / (steps * count)
    return jnp.sum(weights * (states - stepped) ** 2, axis=(0, 1), keepdims=True)


def send_on(start, map_ref, sent_ref):
    sent_ref[...] = jnp.broadcast_to(through(start, map_ref), sent_ref.shape)


def fetch_kernel(
    inputs_hbm, start_hbm, in_weight_hbm, weight_hbm, update_bias_hbm, reset_bias_hbm, cand_bias_hbm,
    rec_bias_hbm,
    wide_ref, in_weight_ref, weight_ref, bias_ref, consts_ref,
    inputs_ref, start_ref, rec_bias_ref, sems
):
    units = weight_ref.shape[0]
    moves = [
        (inputs_hbm, inputs_ref), (in_weight_hbm, in_weight_ref), (weight_hbm, weight_ref),
        (update_bias_hbm, bias_ref.at[:, pl.ds(0, units)]),
        (reset_bias_hbm, bias_ref.at[:, pl.ds(units, units)]),
        (cand_bias_hbm, bias_ref.at[:, pl.ds(2 * units, units)]),
        (start_hbm, start_ref), (rec_bias_hbm, rec_bias_ref),
    ]
    copies = [pltpu.make_async_copy(src, dst, sems.at[i]) for i, (src, dst) in enumerate(moves)]
    for copy in copies:
        copy.start()
    for copy in copies:
        copy.wait()
    wide_ref[...] = inputs_ref[...].astype(F32)
    consts_ref[0:1, :] = start_ref[...]
    consts_ref[1:2, :] = rec_bias_ref[...]
    consts_ref[2:, :] = jnp.zeros((6, units), F32)


def first_kernel(at_front, consts_ref, in_weight_ref, bias_ref, weight_ref, *refs):
    shares, refs = refs[:SPAN], refs[SPAN:]
    gates_ref, sums_ref, prev_ref, mats_ref, vecs_ref, sent_ref, map_ref, held_ref, *coef_refs = refs
    steps, units = prev_ref.shape
    place = lax.rem(lax.axis_index("tm"), SPAN)

    @pl.when((group() == 0) == at_front)
    def _():
        sums_ref[...] = jnp.zeros(sums_ref.shape, F32)
        for k in range(SPAN):
            held_ref[k] = shares[k][...]
        inputs = jnp.concatenate([held_ref[place ^ j] for j in range(SPAN)], axis=0).astype(BF16)
        gates = jnp.dot(inputs, in_weight_ref[...], preferred_element_type=F32) + bias_ref[...]
        gates_ref[...] = gates
        start = consts_ref[0:1, :]
        previous = jnp.zeros((steps, units), F32)
        if at_front:
            row = lax.broadcasted_iota(jnp.int32, (steps, units), 0)
            previous = jnp.where(row == 0, start, 0.0)
        prev_ref[...] = previous
        parts = cell(gates, previous, weight_ref[...], consts_ref[1:2, :])
        fold(parts, prev_ref, weight_ref, coef_refs, mats_ref, vecs_ref, map_ref)
        if at_front:
            send_on(start, map_ref, sent_ref)


def hop_kernel(sent_first_ref, map_ref, arrived_ref, sent_ref):
    state = through(arrived_ref[0:1, :], map_ref)
    sent_ref[...] = jnp.where(group() == 0, sent_first_ref[...], state)


def middle_kernel(
    newton, at_front, start_ref, consts_ref, gates_ref, weight_ref, old_prev_ref, old_mats_ref, old_vecs_ref,
    sums_ref, new_sums_ref, new_prev_ref, mats_ref, vecs_ref, sent_ref, map_ref, states_ref, *coef_refs
):
    @pl.when((group() == 0) == at_front)
    def _():
        entering = start_ref[0:1, :]
        unfold(entering, old_prev_ref, old_mats_ref, old_vecs_ref, states_ref)
        shift_in(entering, states_ref, new_prev_ref)
        parts = cell(gates_ref[...], new_prev_ref[...], weight_ref[...], consts_ref[1:2, :])
        add_sum(newton, sums_ref, states_ref, parts, new_sums_ref)
        fold(parts, new_prev_ref, weight_ref, coef_refs, mats_ref, vecs_ref, map_ref)
        if at_front:
            send_on(entering, map_ref, sent_ref)


def add_sum(newton, sums_ref, states_ref, parts, new_sums_ref):
    done = weighted_square(states_ref[...], parts[4])
    lane = lax.broadcasted_iota(jnp.int32, new_sums_ref.shape, 1)
    new_sums_ref[...] = jnp.where(lane == newton, done, sums_ref[...])


def last_kernel(newton, sides, consts_ref, weight_ref, *refs):
    sides_refs, refs = [refs[6 * i : 6 * i + 6] for i in range(sides)], refs[6 * sides :]
    out_ref, new_sums_ref, prev_ref, states_ref = refs
    for side, (start_ref, gates_ref, sums_ref, old_prev_ref, old_mats_ref, old_vecs_ref) in enumerate(sides_refs):

        @pl.when((group() == 0) == (side == 0))
        def _():
            entering = start_ref[0:1, :]
            unfold(entering, old_prev_ref, old_mats_ref, old_vecs_ref, states_ref)
            shift_in(entering, states_ref, prev_ref)
            parts = cell(gates_ref[...], prev_ref[...], weight_ref[...], consts_ref[1:2, :])
            add_sum(newton, sums_ref, states_ref, parts, new_sums_ref)

    share = out_ref.shape[0]
    first = pl.multiple_of(lax.rem(lax.axis_index("tm"), SPAN) * share, share)
    out_ref[...] = states_ref[pl.ds(first, share), :]


def call(kernel, args, outs, scratch=(), space=pltpu.VMEM):
    args = [pltpu.with_memory_space_constraint(arg, space) for arg in args]
    return pl.pallas_call(
        kernel,
        out_shape=[jax.ShapeDtypeStruct(o, F32) if isinstance(o, tuple) else o for o in outs],
        in_specs=[pl.BlockSpec(memory_space=space)] * len(args),
        out_specs=[pl.BlockSpec(memory_space=pltpu.VMEM)] * len(outs),
        scratch_shapes=[pltpu.VMEM(one, F32) if isinstance(one, tuple) else one for one in scratch],
        compiler_params=pltpu.CompilerParams(vmem_limit_bytes=16 * 1024 * 1024),
    )(*args)


def exchanged(value, axis, by):
    return lax.ppermute(value, axis, [(i, i ^ by) for i in range(lax.axis_size(axis))])


def summed(value, axis, by=1):
    count = lax.axis_size(axis)
    while by < count:
        radix = min(4, count // by)
        terms = [value] + [exchanged(value, axis, k * by) for k in range(1, radix)]
        while len(terms) > 1:
            terms = [a + b for a, b in zip(terms[0::2], terms[1::2])]
        value = terms[0]
        by *= radix
    return value


def carry(sent, own_map):
    count = lax.axis_size("tm")
    onward = [(i, i + SPAN) for i in range(count - SPAN)]
    arrived = lax.ppermute(sent, "tm", onward)
    for _ in range(count // SPAN - 2):
        (further,) = call(hop_kernel, [sent, *own_map, arrived], [sent.shape])
        arrived = lax.ppermute(further, "tm", onward)
    return arrived


def per_device(
    inputs, h_start, in_weight, rec_weight, update_bias, reset_bias, cand_bias, rec_bias
):
    share, sequences = inputs.shape[0], inputs.shape[1]
    units = rec_weight.shape[0]
    row = lambda value: value.reshape(1, units)
    steps = share * SPAN
    slots = steps + CHAINS
    rows, wide = (steps, units), (steps, 3 * units)
    sides = min(2, lax.axis_size("tm") // SPAN)
    fold_outs = [(8, units), rows, (slots, units, units), (slots, units)]
    coefs = [rows] * 5
    state_row, map_rows = (8, units), (units + 8, units)
    further = lax.axis_size("tm") // SPAN > 2
    ends = [([state_row], [map_rows])]
    if sides > 1:
        ends.append(([state_row, map_rows], []) if further else ([], [state_row, map_rows]))
    own, in_rows, weight, bias, consts = call(
        fetch_kernel,
        [inputs.reshape(share, -1), h_start, in_weight, rec_weight, row(update_bias), row(reset_bias),
         row(cand_bias), row(rec_bias)],
        [(share, units), jax.ShapeDtypeStruct(in_weight.shape, BF16), rec_weight.shape, (1, 3 * units),
         (8, units)],
        [pltpu.VMEM((share, units), BF16), (1, units), (1, units), pltpu.SemaphoreType.DMA((8,))],
        space=pltpu.HBM,
    )
    shares = [own] + [exchanged(own, "tm", k) for k in range(1, SPAN)]
    held = []
    for side, (out, kept) in enumerate(ends):
        held.append(call(
            functools.partial(first_kernel, side == 0), [consts, in_rows, bias, weight, *shares],
            [wide] + fold_outs + out, kept + [(SPAN, share, units)] + coefs,
        ))
    for newton in range(ITERS):
        starts = [consts] + [carry(held[0][5], held[-1][6:])] * (sides - 1)
        if newton < ITERS - 1:
            held = [
                held[side][:1] + call(
                    functools.partial(middle_kernel, newton, side == 0),
                    [starts[side], consts, held[side][0], weight, *held[side][2:5], held[side][1]],
                    fold_outs + out, kept + [rows] + coefs,
                )
                for side, (out, kept) in enumerate(ends)
            ]
        else:
            args = [one for side in range(sides) for one in (starts[side], *held[side][:5])]
            states, total = call(
                functools.partial(last_kernel, newton, sides), [consts, weight, *args],
                [(share, units), (8, units)], [rows, rows],
            )
    totals = summed(summed(total, "batch"), "tm", SPAN)[0, :ITERS]
    denom = lax.axis_size("batch") * sequences * units * (share * lax.axis_size("tm") + 1) / 2.0
    residual_norms = jnp.sqrt(totals / denom + 1e-06)
    return (states.reshape(share, sequences, units), residual_norms)


def solution(mesh):
    in_specs = (P("tm", "batch", None), P("batch", None), P(), P(), P(), P(), P(), P())
    out_specs = (P("tm", "batch", None), P())
    return jax.shard_map(
        per_device, mesh=mesh, in_specs=in_specs, out_specs=out_specs, check_vma=False
    )
```

```python
import functools

import jax
import jax.numpy as jnp
from jax import lax
from jax.experimental import pallas as pl
from jax.experimental.pallas import tpu as pltpu
from jax.sharding import PartitionSpec as P

ITERS = 2
SPAN = 4
CHAINS = 8
PAD = 16
F32 = jnp.float32
BF16 = jnp.bfloat16


def halves(value):
    high = value.astype(BF16)
    return high, (value - high.astype(F32)).astype(BF16)


def paired_rows(value):
    return jnp.concatenate(halves(value), axis=1)


def paired_cols(value):
    both = jnp.concatenate(halves(value), axis=1)
    return jnp.concatenate([both, both], axis=0)


def product(rows, cols):
    width = cols.shape[1]
    both = jnp.dot(paired_rows(rows), paired_cols(cols), preferred_element_type=F32)
    return both[:, :width] + both[:, width:]


def as_column(row):
    units = row.shape[1]
    return jnp.broadcast_to(row, (units, units)).T


def row_times(column, matrix):
    return jnp.sum(column * matrix, axis=0, keepdims=True)


def cell(gates, previous, rec_weight, rec_bias):
    units = previous.shape[1]
    rec = product(previous, rec_weight)
    update = jax.nn.sigmoid(gates[:, :units] + rec[:, :units])
    reset = jax.nn.sigmoid(gates[:, units : 2 * units] + rec[:, units : 2 * units])
    recur = rec[:, 2 * units :] + rec_bias
    cand = jnp.tanh(gates[:, 2 * units :] + reset * recur)
    stepped = (1.0 - update) * cand + update * previous
    return update, reset, recur, cand, stepped


def group():
    return lax.axis_index("tm") // SPAN


def through(state, one_map):
    units = state.shape[1]
    column = as_column(state - one_map[units + 1 : units + 2, :])
    return row_times(column, one_map[:units, :]) + one_map[units : units + 1, :]


def joins(steps):
    size = steps // CHAINS
    slots = {(b, 1): (b + 1) * size - 1 for b in range(CHAINS)}
    free, span = steps, 2
    while span <= CHAINS:
        for b in range(0, CHAINS, span):
            slots[(b, span)] = free
            free += 1
        span *= 2
    return slots


def fold(parts, prev_ref, weight_ref, coef_refs, mats_ref, vecs_ref, map_ref):
    update, reset, recur, cand, stepped = parts
    steps, units = update.shape
    size = steps // CHAINS
    previous = prev_ref[...]
    update_ref, coef_update_ref, coef_reset_ref, coef_cand_ref, step_ref = coef_refs
    common = (1.0 - update) * (1.0 - cand * cand)
    update_ref[...] = update
    coef_update_ref[...] = (previous - cand) * update * (1.0 - update)
    coef_reset_ref[...] = common * recur * reset * (1.0 - reset)
    coef_cand_ref[...] = common * reset
    step_ref[...] = stepped
    row = lax.broadcasted_iota(jnp.int32, (units, units), 0)
    col = lax.broadcasted_iota(jnp.int32, (units, units), 1)

    def slope(t):
        return (
            weight_ref[:, :units] * coef_update_ref[t : t + 1, :]
            + weight_ref[:, units : 2 * units] * coef_reset_ref[t : t + 1, :]
            + weight_ref[:, 2 * units :] * coef_cand_ref[t : t + 1, :]
        )

    def stacked(mat, vec):
        return jnp.concatenate([mat, jnp.broadcast_to(vec, (PAD, units))], axis=0)

    for block in range(CHAINS):
        t = block * size
        mats_ref[t] = slope(t) + jnp.where(row == col, update_ref[t : t + 1, :], 0.0)
        vecs_ref[t : t + 1, :] = step_ref[t : t + 1, :]

    for inner in range(1, size):
        for block in range(CHAINS):
            t = block * size + inner
            before = stacked(mats_ref[t - 1], vecs_ref[t - 1 : t, :] - prev_ref[t : t + 1, :])
            after = product(before, slope(t)) + before * update_ref[t : t + 1, :]
            mats_ref[t] = after[:units]
            vecs_ref[t : t + 1, :] = after[units : units + 1] + step_ref[t : t + 1, :]

    slots = joins(steps)
    for (first, span), slot in slots.items():
        if span > 1:
            second = first + span // 2
            early, late = slots[(first, span // 2)], slots[(second, span // 2)]
            shifted = vecs_ref[early : early + 1, :] - prev_ref[second * size : second * size + 1, :]
            after = product(stacked(mats_ref[early], shifted), mats_ref[late])
            mats_ref[slot] = after[:units]
            vecs_ref[slot : slot + 1, :] = after[units : units + 1] + vecs_ref[late : late + 1, :]
    last = slots[(0, CHAINS)]
    map_ref[:units, :] = mats_ref[last]
    map_ref[units : units + 1, :] = vecs_ref[last : last + 1, :]
    map_ref[units + 1 : units + 2, :] = prev_ref[0:1, :]
    map_ref[units + 2 :, :] = jnp.zeros((6, units), F32)


def unfold(entering, prev_ref, mats_ref, vecs_ref, out_ref):
    steps = prev_ref.shape[0]
    size = steps // CHAINS
    slots = joins(steps)
    starts = {0: entering}
    for b in sorted(range(CHAINS), key=lambda b: (bin(b).count("1"), -b)):
        t = b * size
        column = as_column(starts[b] - prev_ref[t : t + 1, :])
        span = 1
        while b % (2 * span) == 0 and b + span < CHAINS:
            slot = slots[(b, span)]
            starts[b + span] = row_times(column, mats_ref[slot]) + vecs_ref[slot : slot + 1, :]
            span *= 2
        for inner in range(size):
            state = row_times(column, mats_ref[t + inner]) + vecs_ref[t + inner : t + inner + 1, :]
            out_ref[t + inner : t + inner + 1, :] = state


def shift_in(entering, states_ref, prev_ref):
    steps = states_ref.shape[0]
    prev_ref[0:1, :] = entering
    prev_ref[1:steps, :] = states_ref[0 : steps - 1, :]


def weighted_square(states, stepped):
    steps = states.shape[0]
    count = lax.axis_size("tm") // SPAN
    position = group() * steps + lax.broadcasted_iota(jnp.int32, states.shape, 0)
    weights = (position.astype(F32) + 1.0) / (steps * count)
    return jnp.sum(weights * (states - stepped) ** 2, axis=(0, 1), keepdims=True)


def send_on(start, map_ref, sent_ref):
    sent_ref[...] = jnp.broadcast_to(through(start, map_ref), sent_ref.shape)


def fetch_kernel(
    inputs_hbm, start_hbm, in_weight_hbm, weight_hbm, update_bias_hbm, reset_bias_hbm, cand_bias_hbm,
    rec_bias_hbm,
    wide_ref, in_weight_ref, weight_ref, bias_ref, consts_ref,
    inputs_ref, start_ref, rec_bias_ref, sems
):
    units = weight_ref.shape[0]
    moves = [
        (inputs_hbm, inputs_ref), (in_weight_hbm, in_weight_ref), (weight_hbm, weight_ref),
        (update_bias_hbm, bias_ref.at[:, pl.ds(0, units)]),
        (reset_bias_hbm, bias_ref.at[:, pl.ds(units, units)]),
        (cand_bias_hbm, bias_ref.at[:, pl.ds(2 * units, units)]),
        (start_hbm, start_ref), (rec_bias_hbm, rec_bias_ref),
    ]
    copies = [pltpu.make_async_copy(src, dst, sems.at[i]) for i, (src, dst) in enumerate(moves)]
    for copy in copies:
        copy.start()
    for copy in copies:
        copy.wait()
    wide_ref[...] = inputs_ref[...].astype(F32)
    consts_ref[0:1, :] = start_ref[...]
    consts_ref[1:2, :] = rec_bias_ref[...]
    consts_ref[2:, :] = jnp.zeros((6, units), F32)


def first_kernel(at_front, consts_ref, in_weight_ref, bias_ref, weight_ref, *refs):
    shares, refs = refs[:SPAN], refs[SPAN:]
    gates_ref, sums_ref, prev_ref, mats_ref, vecs_ref, sent_ref, map_ref, held_ref, *coef_refs = refs
    steps, units = prev_ref.shape
    place = lax.rem(lax.axis_index("tm"), SPAN)

    @pl.when((group() == 0) == at_front)
    def _():
        sums_ref[...] = jnp.zeros(sums_ref.shape, F32)
        for k in range(SPAN):
            held_ref[k] = shares[SPAN - 1 - k][...]
        inputs = jnp.concatenate([held_ref[place ^ j] for j in range(SPAN)], axis=0).astype(BF16)
        gates = jnp.dot(inputs, in_weight_ref[...], preferred_element_type=F32) + bias_ref[...]
        gates_ref[...] = gates
        start = consts_ref[0:1, :]
        previous = jnp.zeros((steps, units), F32)
        if at_front:
            row = lax.broadcasted_iota(jnp.int32, (steps, units), 0)
            previous = jnp.where(row == 0, start, 0.0)
        prev_ref[...] = previous
        parts = cell(gates, previous, weight_ref[...], consts_ref[1:2, :])
        fold(parts, prev_ref, weight_ref, coef_refs, mats_ref, vecs_ref, map_ref)
        if at_front:
            send_on(start, map_ref, sent_ref)


def hop_kernel(sent_first_ref, map_ref, arrived_ref, sent_ref):
    state = through(arrived_ref[0:1, :], map_ref)
    sent_ref[...] = jnp.where(group() == 0, sent_first_ref[...], state)


def middle_kernel(
    newton, at_front, start_ref, consts_ref, gates_ref, weight_ref, old_prev_ref, old_mats_ref, old_vecs_ref,
    sums_ref, new_sums_ref, new_prev_ref, mats_ref, vecs_ref, sent_ref, map_ref, states_ref, *coef_refs
):
    @pl.when((group() == 0) == at_front)
    def _():
        entering = start_ref[0:1, :]
        unfold(entering, old_prev_ref, old_mats_ref, old_vecs_ref, states_ref)
        shift_in(entering, states_ref, new_prev_ref)
        parts = cell(gates_ref[...], new_prev_ref[...], weight_ref[...], consts_ref[1:2, :])
        add_sum(newton, sums_ref, states_ref, parts, new_sums_ref)
        fold(parts, new_prev_ref, weight_ref, coef_refs, mats_ref, vecs_ref, map_ref)
        if at_front:
            send_on(entering, map_ref, sent_ref)


def add_sum(newton, sums_ref, states_ref, parts, new_sums_ref):
    done = weighted_square(states_ref[...], parts[4])
    lane = lax.broadcasted_iota(jnp.int32, new_sums_ref.shape, 1)
    new_sums_ref[...] = jnp.where(lane == newton, done, sums_ref[...])


def last_kernel(newton, sides, consts_ref, weight_ref, *refs):
    sides_refs, refs = [refs[6 * i : 6 * i + 6] for i in range(sides)], refs[6 * sides :]
    out_ref, new_sums_ref, prev_ref, states_ref = refs
    for side, (start_ref, gates_ref, sums_ref, old_prev_ref, old_mats_ref, old_vecs_ref) in enumerate(sides_refs):

        @pl.when((group() == 0) == (side == 0))
        def _():
            entering = start_ref[0:1, :]
            unfold(entering, old_prev_ref, old_mats_ref, old_vecs_ref, states_ref)
            shift_in(entering, states_ref, prev_ref)
            parts = cell(gates_ref[...], prev_ref[...], weight_ref[...], consts_ref[1:2, :])
            add_sum(newton, sums_ref, states_ref, parts, new_sums_ref)

    share = out_ref.shape[0]
    first = pl.multiple_of(lax.rem(lax.axis_index("tm"), SPAN) * share, share)
    out_ref[...] = states_ref[pl.ds(first, share), :]


def call(kernel, args, outs, scratch=(), space=pltpu.VMEM):
    args = [pltpu.with_memory_space_constraint(arg, space) for arg in args]
    return pl.pallas_call(
        kernel,
        out_shape=[jax.ShapeDtypeStruct(o, F32) if isinstance(o, tuple) else o for o in outs],
        in_specs=[pl.BlockSpec(memory_space=space)] * len(args),
        out_specs=[pl.BlockSpec(memory_space=pltpu.VMEM)] * len(outs),
        scratch_shapes=[pltpu.VMEM(one, F32) if isinstance(one, tuple) else one for one in scratch],
        compiler_params=pltpu.CompilerParams(vmem_limit_bytes=16 * 1024 * 1024),
    )(*args)


def exchanged(value, axis, by):
    return lax.ppermute(value, axis, [(i, i ^ by) for i in range(lax.axis_size(axis))])


def summed(value, axis, by=1):
    count = lax.axis_size(axis)
    while by < count:
        radix = min(4, count // by)
        terms = [exchanged(value, axis, k * by) for k in range(radix - 1, 0, -1)] + [value]
        while len(terms) > 1:
            terms = [a + b for a, b in zip(terms[0::2], terms[1::2])]
        value = terms[0]
        by *= radix
    return value


def carry(sent, own_map):
    count = lax.axis_size("tm")
    onward = [(i, i + SPAN) for i in range(count - SPAN)]
    arrived = lax.ppermute(sent, "tm", onward)
    for _ in range(count // SPAN - 2):
        (further,) = call(hop_kernel, [sent, *own_map, arrived], [sent.shape])
        arrived = lax.ppermute(further, "tm", onward)
    return arrived


def per_device(
    inputs, h_start, in_weight, rec_weight, update_bias, reset_bias, cand_bias, rec_bias
):
    share, sequences = inputs.shape[0], inputs.shape[1]
    units = rec_weight.shape[0]
    row = lambda value: value.reshape(1, units)
    steps = share * SPAN
    slots = steps + CHAINS
    rows, wide = (steps, units), (steps, 3 * units)
    sides = min(2, lax.axis_size("tm") // SPAN)
    fold_outs = [(8, units), rows, (slots, units, units), (slots, units)]
    coefs = [rows] * 5
    state_row, map_rows = (8, units), (units + 8, units)
    further = lax.axis_size("tm") // SPAN > 2
    ends = [([state_row], [map_rows])]
    if sides > 1:
        ends.append(([state_row, map_rows], []) if further else ([], [state_row, map_rows]))
    own, in_rows, weight, bias, consts = call(
        fetch_kernel,
        [inputs.reshape(share, -1), h_start, in_weight, rec_weight, row(update_bias), row(reset_bias),
         row(cand_bias), row(rec_bias)],
        [(share, units), jax.ShapeDtypeStruct(in_weight.shape, BF16), rec_weight.shape, (1, 3 * units),
         (8, units)],
        [pltpu.VMEM((share, units), BF16), (1, units), (1, units), pltpu.SemaphoreType.DMA((8,))],
        space=pltpu.HBM,
    )
    shares = [exchanged(own, "tm", k) for k in range(SPAN - 1, 0, -1)] + [own]
    held = []
    for side, (out, kept) in enumerate(ends):
        held.append(call(
            functools.partial(first_kernel, side == 0), [consts, in_rows, bias, weight, *shares],
            [wide] + fold_outs + out, kept + [(SPAN, share, units)] + coefs,
        ))
    for newton in range(ITERS):
        starts = [consts] + [carry(held[0][5], held[-1][6:])] * (sides - 1)
        if newton < ITERS - 1:
            held = [
                held[side][:1] + call(
                    functools.partial(middle_kernel, newton, side == 0),
                    [starts[side], consts, held[side][0], weight, *held[side][2:5], held[side][1]],
                    fold_outs + out, kept + [rows] + coefs,
                )
                for side, (out, kept) in enumerate(ends)
            ]
        else:
            args = [one for side in range(sides) for one in (starts[side], *held[side][:5])]
            states, total = call(
                functools.partial(last_kernel, newton, sides), [consts, weight, *args],
                [(share, units), (8, units)], [rows, rows],
            )
    totals = summed(summed(total, "batch"), "tm", SPAN)[0, :ITERS]
    denom = lax.axis_size("batch") * sequences * units * (share * lax.axis_size("tm") + 1) / 2.0
    residual_norms = jnp.sqrt(totals / denom + 1e-06)
    return (states.reshape(share, sequences, units), residual_norms)


def solution(mesh):
    in_specs = (P("tm", "batch", None), P("batch", None), P(), P(), P(), P(), P(), P())
    out_specs = (P("tm", "batch", None), P())
    return jax.shard_map(
        per_device, mesh=mesh, in_specs=in_specs, out_specs=out_specs, check_vma=False
    )
```

```python
import functools

import jax
import jax.numpy as jnp
from jax import lax
from jax.experimental import pallas as pl
from jax.experimental.pallas import tpu as pltpu
from jax.sharding import PartitionSpec as P

ITERS = 2
SPAN = 4
CHAINS = 8
PAD = 16
F32 = jnp.float32
BF16 = jnp.bfloat16


def halves(value):
    high = value.astype(BF16)
    return high, (value - high.astype(F32)).astype(BF16)


def paired_rows(value):
    return jnp.concatenate(halves(value), axis=1)


def paired_cols(value):
    both = jnp.concatenate(halves(value), axis=1)
    return jnp.concatenate([both, both], axis=0)


def product(rows, cols):
    width = cols.shape[1]
    both = jnp.dot(paired_rows(rows), paired_cols(cols), preferred_element_type=F32)
    return both[:, :width] + both[:, width:]


def as_column(row):
    units = row.shape[1]
    return jnp.broadcast_to(row, (units, units)).T


def row_times(column, matrix):
    return jnp.sum(column * matrix, axis=0, keepdims=True)


def cell(gates, previous, rec_weight, rec_bias):
    units = previous.shape[1]
    rec = product(previous, rec_weight)
    update = jax.nn.sigmoid(gates[:, :units] + rec[:, :units])
    reset = jax.nn.sigmoid(gates[:, units : 2 * units] + rec[:, units : 2 * units])
    recur = rec[:, 2 * units :] + rec_bias
    cand = jnp.tanh(gates[:, 2 * units :] + reset * recur)
    stepped = (1.0 - update) * cand + update * previous
    return update, reset, recur, cand, stepped


def group():
    return lax.axis_index("tm") // SPAN


def through(state, one_map):
    units = state.shape[1]
    column = as_column(state - one_map[units + 1 : units + 2, :])
    return row_times(column, one_map[:units, :]) + one_map[units : units + 1, :]


def joins(steps):
    size = steps // CHAINS
    slots = {(b, 1): (b + 1) * size - 1 for b in range(CHAINS)}
    free, span = steps, 2
    while span <= CHAINS:
        for b in range(0, CHAINS, span):
            slots[(b, span)] = free
            free += 1
        span *= 2
    return slots


def fold(parts, prev_ref, weight_ref, coef_refs, mats_ref, vecs_ref, map_ref):
    update, reset, recur, cand, stepped = parts
    steps, units = update.shape
    size = steps // CHAINS
    previous = prev_ref[...]
    update_ref, coef_update_ref, coef_reset_ref, coef_cand_ref, step_ref = coef_refs
    common = (1.0 - update) * (1.0 - cand * cand)
    update_ref[...] = update
    coef_update_ref[...] = (previous - cand) * update * (1.0 - update)
    coef_reset_ref[...] = common * recur * reset * (1.0 - reset)
    coef_cand_ref[...] = common * reset
    step_ref[...] = stepped
    row = lax.broadcasted_iota(jnp.int32, (units, units), 0)
    col = lax.broadcasted_iota(jnp.int32, (units, units), 1)

    def slope(t):
        return (
            weight_ref[:, :units] * coef_update_ref[t : t + 1, :]
            + weight_ref[:, units : 2 * units] * coef_reset_ref[t : t + 1, :]
            + weight_ref[:, 2 * units :] * coef_cand_ref[t : t + 1, :]
        )

    def stacked(mat, vec):
        return jnp.concatenate([mat, jnp.broadcast_to(vec, (PAD, units))], axis=0)

    for block in range(CHAINS):
        t = block * size
        mats_ref[t] = slope(t) + jnp.where(row == col, update_ref[t : t + 1, :], 0.0)
        vecs_ref[t : t + 1, :] = step_ref[t : t + 1, :]

    for inner in range(1, size):
        for block in range(CHAINS):
            t = block * size + inner
            before = stacked(mats_ref[t - 1], vecs_ref[t - 1 : t, :] - prev_ref[t : t + 1, :])
            after = product(before, slope(t)) + before * update_ref[t : t + 1, :]
            mats_ref[t] = after[:units]
            vecs_ref[t : t + 1, :] = after[units : units + 1] + step_ref[t : t + 1, :]

    slots = joins(steps)
    for (first, span), slot in slots.items():
        if span > 1:
            second = first + span // 2
            early, late = slots[(first, span // 2)], slots[(second, span // 2)]
            shifted = vecs_ref[early : early + 1, :] - prev_ref[second * size : second * size + 1, :]
            after = product(stacked(mats_ref[early], shifted), mats_ref[late])
            mats_ref[slot] = after[:units]
            vecs_ref[slot : slot + 1, :] = after[units : units + 1] + vecs_ref[late : late + 1, :]
    last = slots[(0, CHAINS)]
    map_ref[:units, :] = mats_ref[last]
    map_ref[units : units + 1, :] = vecs_ref[last : last + 1, :]
    map_ref[units + 1 : units + 2, :] = prev_ref[0:1, :]
    map_ref[units + 2 :, :] = jnp.zeros((6, units), F32)


def unfold(entering, prev_ref, mats_ref, vecs_ref, out_ref):
    steps = prev_ref.shape[0]
    size = steps // CHAINS
    slots = joins(steps)
    starts = {0: entering}
    for b in sorted(range(CHAINS), key=lambda b: (bin(b).count("1"), -b)):
        t = b * size
        column = as_column(starts[b] - prev_ref[t : t + 1, :])
        span = 1
        while b % (2 * span) == 0 and b + span < CHAINS:
            slot = slots[(b, span)]
            starts[b + span] = row_times(column, mats_ref[slot]) + vecs_ref[slot : slot + 1, :]
            span *= 2
        for inner in range(size):
            state = row_times(column, mats_ref[t + inner]) + vecs_ref[t + inner : t + inner + 1, :]
            out_ref[t + inner : t + inner + 1, :] = state


def shift_in(entering, states_ref, prev_ref):
    steps = states_ref.shape[0]
    prev_ref[0:1, :] = entering
    prev_ref[1:steps, :] = states_ref[0 : steps - 1, :]


def weighted_square(states, stepped):
    steps = states.shape[0]
    count = lax.axis_size("tm") // SPAN
    position = group() * steps + lax.broadcasted_iota(jnp.int32, states.shape, 0)
    weights = (position.astype(F32) + 1.0) / (steps * count)
    return jnp.sum(weights * (states - stepped) ** 2, axis=(0, 1), keepdims=True)


def send_on(start, map_ref, sent_ref):
    sent_ref[...] = jnp.broadcast_to(through(start, map_ref), sent_ref.shape)


def fetch_kernel(
    inputs_hbm, start_hbm, in_weight_hbm, weight_hbm, update_bias_hbm, reset_bias_hbm, cand_bias_hbm,
    rec_bias_hbm,
    wide_ref, in_weight_ref, weight_ref, bias_ref, consts_ref,
    inputs_ref, start_ref, rec_bias_ref, sems
):
    units = weight_ref.shape[0]
    moves = [
        (inputs_hbm, inputs_ref), (in_weight_hbm, in_weight_ref), (weight_hbm, weight_ref),
        (update_bias_hbm, bias_ref.at[:, pl.ds(0, units)]),
        (reset_bias_hbm, bias_ref.at[:, pl.ds(units, units)]),
        (cand_bias_hbm, bias_ref.at[:, pl.ds(2 * units, units)]),
        (start_hbm, start_ref), (rec_bias_hbm, rec_bias_ref),
    ]
    copies = [pltpu.make_async_copy(src, dst, sems.at[i]) for i, (src, dst) in enumerate(moves)]
    for copy in copies:
        copy.start()
    for copy in copies:
        copy.wait()
    wide_ref[...] = inputs_ref[...].astype(F32)
    consts_ref[0:1, :] = start_ref[...]
    consts_ref[1:2, :] = rec_bias_ref[...]
    consts_ref[2:, :] = jnp.zeros((6, units), F32)


def first_kernel(at_front, consts_ref, in_weight_ref, bias_ref, weight_ref, *refs):
    shares, refs = refs[:SPAN], refs[SPAN:]
    gates_ref, sums_ref, prev_ref, mats_ref, vecs_ref, sent_ref, map_ref, held_ref, *coef_refs = refs
    steps, units = prev_ref.shape
    place = lax.rem(lax.axis_index("tm"), SPAN)

    @pl.when((group() == 0) == at_front)
    def _():
        sums_ref[...] = jnp.zeros(sums_ref.shape, F32)
        for k in range(SPAN):
            held_ref[k] = shares[SPAN - 1 - k][...]
        inputs = jnp.concatenate([held_ref[place ^ j] for j in range(SPAN)], axis=0).astype(BF16)
        gates = jnp.dot(inputs, in_weight_ref[...], preferred_element_type=F32) + bias_ref[...]
        gates_ref[...] = gates
        start = consts_ref[0:1, :]
        previous = jnp.zeros((steps, units), F32)
        if at_front:
            row = lax.broadcasted_iota(jnp.int32, (steps, units), 0)
            previous = jnp.where(row == 0, start, 0.0)
        prev_ref[...] = previous
        parts = cell(gates, previous, weight_ref[...], consts_ref[1:2, :])
        fold(parts, prev_ref, weight_ref, coef_refs, mats_ref, vecs_ref, map_ref)
        if at_front:
            send_on(start, map_ref, sent_ref)


def hop_kernel(sent_first_ref, map_ref, arrived_ref, sent_ref):
    state = through(arrived_ref[0:1, :], map_ref)
    sent_ref[...] = jnp.where(group() == 0, sent_first_ref[...], state)


def middle_kernel(
    newton, at_front, start_ref, consts_ref, gates_ref, weight_ref, old_prev_ref, old_mats_ref, old_vecs_ref,
    sums_ref, new_sums_ref, new_prev_ref, mats_ref, vecs_ref, sent_ref, map_ref, states_ref, *coef_refs
):
    @pl.when((group() == 0) == at_front)
    def _():
        entering = start_ref[0:1, :]
        unfold(entering, old_prev_ref, old_mats_ref, old_vecs_ref, states_ref)
        shift_in(entering, states_ref, new_prev_ref)
        parts = cell(gates_ref[...], new_prev_ref[...], weight_ref[...], consts_ref[1:2, :])
        add_sum(newton, sums_ref, states_ref, parts, new_sums_ref)
        fold(parts, new_prev_ref, weight_ref, coef_refs, mats_ref, vecs_ref, map_ref)
        if at_front:
            send_on(entering, map_ref, sent_ref)


def add_sum(newton, sums_ref, states_ref, parts, new_sums_ref):
    done = weighted_square(states_ref[...], parts[4])
    lane = lax.broadcasted_iota(jnp.int32, (1, states_ref.shape[1]), 1)
    sums = jnp.where(lane == newton, done, sums_ref[0:1, :])
    new_sums_ref[...] = jnp.broadcast_to(sums.reshape((1,) * len(new_sums_ref.shape[:-1]) + sums.shape[1:]), new_sums_ref.shape)


def last_kernel(newton, sides, consts_ref, weight_ref, *refs):
    sides_refs, refs = [refs[6 * i : 6 * i + 6] for i in range(sides)], refs[6 * sides :]
    out_ref, new_sums_ref, prev_ref, states_ref = refs
    for side, (start_ref, gates_ref, sums_ref, old_prev_ref, old_mats_ref, old_vecs_ref) in enumerate(sides_refs):

        @pl.when((group() == 0) == (side == 0))
        def _():
            entering = start_ref[0:1, :]
            unfold(entering, old_prev_ref, old_mats_ref, old_vecs_ref, states_ref)
            shift_in(entering, states_ref, prev_ref)
            parts = cell(gates_ref[...], prev_ref[...], weight_ref[...], consts_ref[1:2, :])
            add_sum(newton, sums_ref, states_ref, parts, new_sums_ref)

    share = out_ref.shape[0]
    first = pl.multiple_of(lax.rem(lax.axis_index("tm"), SPAN) * share, share)
    out_ref[...] = states_ref[pl.ds(first, share), :]


def call(kernel, args, outs, scratch=(), space=pltpu.VMEM):
    args = [pltpu.with_memory_space_constraint(arg, space) for arg in args]
    return pl.pallas_call(
        kernel,
        out_shape=[jax.ShapeDtypeStruct(o, F32) if isinstance(o, tuple) else o for o in outs],
        in_specs=[pl.BlockSpec(memory_space=space)] * len(args),
        out_specs=[pl.BlockSpec(memory_space=pltpu.VMEM)] * len(outs),
        scratch_shapes=[pltpu.VMEM(one, F32) if isinstance(one, tuple) else one for one in scratch],
        compiler_params=pltpu.CompilerParams(vmem_limit_bytes=16 * 1024 * 1024),
    )(*args)


def exchanged(value, axis, by):
    return lax.ppermute(value, axis, [(i, i ^ by) for i in range(lax.axis_size(axis))])


def summed(rows, by):
    count, batch = lax.axis_size("tm"), lax.axis_size("batch")
    groups = [[i * batch + j for i in range(place, count, by) for j in range(batch)] for place in range(by)]
    return jnp.sum(lax.all_to_all(rows, ("tm", "batch"), 0, 0, axis_index_groups=groups), axis=0)


def carry(sent, own_map):
    count = lax.axis_size("tm")
    onward = [(i, i + SPAN) for i in range(count - SPAN)]
    arrived = lax.ppermute(sent, "tm", onward)
    for _ in range(count // SPAN - 2):
        (further,) = call(hop_kernel, [sent, *own_map, arrived], [sent.shape])
        arrived = lax.ppermute(further, "tm", onward)
    return arrived


def per_device(
    inputs, h_start, in_weight, rec_weight, update_bias, reset_bias, cand_bias, rec_bias
):
    share, sequences = inputs.shape[0], inputs.shape[1]
    units = rec_weight.shape[0]
    row = lambda value: value.reshape(1, units)
    steps = share * SPAN
    slots = steps + CHAINS
    rows, wide = (steps, units), (steps, 3 * units)
    sides = min(2, lax.axis_size("tm") // SPAN)
    fold_outs = [(8, units), rows, (slots, units, units), (slots, units)]
    coefs = [rows] * 5
    state_row, map_rows = (8, units), (units + 8, units)
    further = lax.axis_size("tm") // SPAN > 2
    ends = [([state_row], [map_rows])]
    if sides > 1:
        ends.append(([state_row, map_rows], []) if further else ([], [state_row, map_rows]))
    own, in_rows, weight, bias, consts = call(
        fetch_kernel,
        [inputs.reshape(share, -1), h_start, in_weight, rec_weight, row(update_bias), row(reset_bias),
         row(cand_bias), row(rec_bias)],
        [(share, units), jax.ShapeDtypeStruct(in_weight.shape, BF16), rec_weight.shape, (1, 3 * units),
         (8, units)],
        [pltpu.VMEM((share, units), BF16), (1, units), (1, units), pltpu.SemaphoreType.DMA((8,))],
        space=pltpu.HBM,
    )
    shares = [exchanged(own, "tm", k) for k in range(SPAN - 1, 0, -1)] + [own]
    held = []
    for side, (out, kept) in enumerate(ends):
        held.append(call(
            functools.partial(first_kernel, side == 0), [consts, in_rows, bias, weight, *shares],
            [wide] + fold_outs + out, kept + [(SPAN, share, units)] + coefs,
        ))
    for newton in range(ITERS):
        starts = [consts] + [carry(held[0][5], held[-1][6:])] * (sides - 1)
        if newton < ITERS - 1:
            held = [
                held[side][:1] + call(
                    functools.partial(middle_kernel, newton, side == 0),
                    [starts[side], consts, held[side][0], weight, *held[side][2:5], held[side][1]],
                    fold_outs + out, kept + [rows] + coefs,
                )
                for side, (out, kept) in enumerate(ends)
            ]
        else:
            args = [one for side in range(sides) for one in (starts[side], *held[side][:5])]
            states, total = call(
                functools.partial(last_kernel, newton, sides), [consts, weight, *args],
                [(share, units), (lax.axis_size("batch") * lax.axis_size("tm") // SPAN, 1, units)], [rows, rows],
            )
    totals = summed(total, SPAN)[0, :ITERS]
    denom = lax.axis_size("batch") * sequences * units * (share * lax.axis_size("tm") + 1) / 2.0
    residual_norms = jnp.sqrt(totals / denom + 1e-06)
    return (states.reshape(share, sequences, units), residual_norms)


def solution(mesh):
    in_specs = (P("tm", "batch", None), P("batch", None), P(), P(), P(), P(), P(), P())
    out_specs = (P("tm", "batch", None), P())
    return jax.shard_map(
        per_device, mesh=mesh, in_specs=in_specs, out_specs=out_specs, check_vma=False
    )
```

```python
import functools

import jax
import jax.numpy as jnp
from jax import lax
from jax.experimental import pallas as pl
from jax.experimental.pallas import tpu as pltpu
from jax.sharding import PartitionSpec as P

ITERS = 2
SPAN = 4
SIZE = 8
PAD = 16
F32 = jnp.float32
BF16 = jnp.bfloat16


def halves(value):
    high = value.astype(BF16)
    return high, (value - high.astype(F32)).astype(BF16)


def paired_rows(value):
    return jnp.concatenate(halves(value), axis=1)


def paired_cols(value):
    both = jnp.concatenate(halves(value), axis=1)
    return jnp.concatenate([both, both], axis=0)


def product(rows, cols):
    width = cols.shape[1]
    both = jnp.dot(paired_rows(rows), paired_cols(cols), preferred_element_type=F32)
    return both[:, :width] + both[:, width:]


def as_column(row):
    units = row.shape[1]
    return jnp.broadcast_to(row, (units, units)).T


def row_times(column, matrix):
    return jnp.sum(column * matrix, axis=0, keepdims=True)


def cell(gates, previous, rec_weight, rec_bias):
    units = previous.shape[1]
    rec = product(previous, rec_weight)
    update = jax.nn.sigmoid(gates[:, :units] + rec[:, :units])
    reset = jax.nn.sigmoid(gates[:, units : 2 * units] + rec[:, units : 2 * units])
    recur = rec[:, 2 * units :] + rec_bias
    cand = jnp.tanh(gates[:, 2 * units :] + reset * recur)
    stepped = (1.0 - update) * cand + update * previous
    return update, reset, recur, cand, stepped


def group():
    return lax.axis_index("tm") // SPAN


def through(state, one_map):
    units = state.shape[1]
    column = as_column(state - one_map[units + 1 : units + 2, :])
    return row_times(column, one_map[:units, :]) + one_map[units : units + 1, :]


def stacked(mat, vec):
    return jnp.concatenate([mat, jnp.broadcast_to(vec, (PAD, mat.shape[1]))], axis=0)


def join(mats, vecs, early, late, base, out):
    after = product(stacked(mats[early], vecs[early : early + 1, :] - base), mats[late])
    units = after.shape[1]
    mats[out] = after[:units]
    vecs[out : out + 1, :] = after[units : units + 1] + vecs[late : late + 1, :]


def layout(share):
    blocks = share // SIZE
    where = {(b, 1): (b + 1) * SIZE - 1 for b in range(blocks)}
    free, span = share, 2
    while span <= blocks:
        for b in range(0, blocks, span):
            where[(b, span)] = free
            free += 1
        span *= 2
    return where, -(-free // 8) * 8


def fold(parts, prev_ref, weight_ref, coef_refs, slots, pieces, share):
    update, reset, recur, cand, stepped = parts
    units = update.shape[1]
    previous = prev_ref[slots[0] * share : (slots[-1] + 1) * share, :]
    update_ref, coef_update_ref, coef_reset_ref, coef_cand_ref, step_ref = coef_refs
    common = (1.0 - update) * (1.0 - cand * cand)
    update_ref[...] = update
    coef_update_ref[...] = (previous - cand) * update * (1.0 - update)
    coef_reset_ref[...] = common * recur * reset * (1.0 - reset)
    coef_cand_ref[...] = common * reset
    step_ref[...] = stepped
    row = lax.broadcasted_iota(jnp.int32, (units, units), 0)
    col = lax.broadcasted_iota(jnp.int32, (units, units), 1)

    def slope(r):
        return (
            weight_ref[:, :units] * coef_update_ref[r : r + 1, :]
            + weight_ref[:, units : 2 * units] * coef_reset_ref[r : r + 1, :]
            + weight_ref[:, 2 * units :] * coef_cand_ref[r : r + 1, :]
        )

    for inner in range(SIZE):
        for i, k in enumerate(slots):
            mats, vecs = pieces[k]
            for t in range(inner, share, SIZE):
                r = i * share + t
                if inner == 0:
                    mats[t] = slope(r) + jnp.where(row == col, update_ref[r : r + 1, :], 0.0)
                    vecs[t : t + 1, :] = step_ref[r : r + 1, :]
                    continue
                taken = prev_ref[k * share + t : k * share + t + 1, :]
                before = stacked(mats[t - 1], vecs[t - 1 : t, :] - taken)
                after = product(before, slope(r)) + before * update_ref[r : r + 1, :]
                mats[t] = after[:units]
                vecs[t : t + 1, :] = after[units : units + 1] + step_ref[r : r + 1, :]
    where, _ = layout(share)
    for (b, span), out in where.items():
        if span > 1:
            second = b + span // 2
            for k in slots:
                base = prev_ref[k * share + second * SIZE : k * share + second * SIZE + 1, :]
                join(*pieces[k], where[(b, span // 2)], where[(second, span // 2)], base, out)


def share_map(share):
    return layout(share)[0][(0, share // SIZE)]


def slot_of(part):
    return lax.rem(lax.axis_index("tm"), SPAN) ^ part


def base_of(prev_ref, part, share):
    return prev_ref[pl.ds(slot_of(part) * share, 1), :]


def fold_shares(prev_ref, pieces, share, tops, top_scratch, map_ref, whole):
    mats, vecs = tops
    held_mats, held_vecs = top_scratch
    at = share_map(share)
    for k in range(SPAN):
        held_mats[k] = pieces[k][0][at]
        held_vecs[k : k + 1, :] = pieces[k][1][at : at + 1, :]
    for part in range(SPAN):
        mats[part] = held_mats[slot_of(part)]
        vecs[part : part + 1, :] = held_vecs[pl.ds(slot_of(part), 1), :]
    join(mats, vecs, 0, 1, base_of(prev_ref, 1, share), 4)
    if whole:
        units = map_ref.shape[1]
        join(mats, vecs, 2, 3, base_of(prev_ref, 3, share), 5)
        join(mats, vecs, 4, 5, base_of(prev_ref, 2, share), 6)
        map_ref[:units, :] = mats[6]
        map_ref[units : units + 1, :] = vecs[6:7, :]
        map_ref[units + 1 : units + 2, :] = base_of(prev_ref, 0, share)
        map_ref[units + 2 :, :] = jnp.zeros((6, units), F32)


def unfold(entering, prev_ref, pieces, tops, share, starts_ref, out_ref):
    top_mats, top_vecs = tops
    starts_ref[0:1, :] = entering
    column = as_column(entering - base_of(prev_ref, 0, share))
    middle = row_times(column, top_mats[4]) + top_vecs[4:5, :]
    starts_ref[1:2, :] = row_times(column, top_mats[0]) + top_vecs[0:1, :]
    starts_ref[2:3, :] = middle
    column = as_column(middle - base_of(prev_ref, 2, share))
    starts_ref[3:4, :] = row_times(column, top_mats[2]) + top_vecs[2:3, :]
    where, _ = layout(share)
    blocks = share // SIZE
    starts = {(0, k): starts_ref[pl.ds(slot_of(k), 1), :] for k in range(SPAN)}
    for b in sorted(range(blocks), key=lambda b: (bin(b).count("1"), -b)):
        for k in range(SPAN):
            mats, vecs = pieces[k]
            t, first = b * SIZE, k * share + b * SIZE
            column = as_column(starts[(b, k)] - prev_ref[first : first + 1, :])
            span = 1
            while b % (2 * span) == 0 and b + span < blocks:
                at = where[(b, span)]
                starts[(b + span, k)] = row_times(column, mats[at]) + vecs[at : at + 1, :]
                span *= 2
            for inner in range(SIZE):
                state = row_times(column, mats[t + inner]) + vecs[t + inner : t + inner + 1, :]
                out_ref[first + inner : first + inner + 1, :] = state


def shift_in(starts_ref, states_ref, prev_ref, share):
    steps = states_ref.shape[0]
    prev_ref[1:steps, :] = states_ref[0 : steps - 1, :]
    for k in range(SPAN):
        prev_ref[k * share : k * share + 1, :] = starts_ref[pl.ds(slot_of(k), 1), :]


def slots_in(refs):
    return [(mats.at[k], vecs.at[k]) for mats, vecs in zip(refs[0::2], refs[1::2]) for k in range(mats.shape[0])]


def weighted_square(states, stepped):
    steps = states.shape[0]
    share = steps // SPAN
    count = lax.axis_size("tm") // SPAN
    row = lax.broadcasted_iota(jnp.int32, states.shape, 0)
    position = group() * steps + slot_of(row // share) * share + row % share
    weights = (position.astype(F32) + 1.0) / (steps * count)
    return jnp.sum(weights * (states - stepped) ** 2, axis=(0, 1), keepdims=True)


def send_on(start, map_ref, sent_ref):
    sent_ref[...] = jnp.broadcast_to(through(start, map_ref), sent_ref.shape)


def fetch_kernel(
    inputs_hbm, start_hbm, in_weight_hbm, weight_hbm, update_bias_hbm, reset_bias_hbm, cand_bias_hbm,
    rec_bias_hbm,
    wide_ref, in_weight_ref, weight_ref, bias_ref, consts_ref,
    inputs_ref, start_ref, rec_bias_ref, sems
):
    units = weight_ref.shape[0]
    moves = [
        (inputs_hbm, inputs_ref), (in_weight_hbm, in_weight_ref), (weight_hbm, weight_ref),
        (update_bias_hbm, bias_ref.at[:, pl.ds(0, units)]),
        (reset_bias_hbm, bias_ref.at[:, pl.ds(units, units)]),
        (cand_bias_hbm, bias_ref.at[:, pl.ds(2 * units, units)]),
        (start_hbm, start_ref), (rec_bias_hbm, rec_bias_ref),
    ]
    copies = [pltpu.make_async_copy(src, dst, sems.at[i]) for i, (src, dst) in enumerate(moves)]
    for copy in copies:
        copy.start()
    for copy in copies:
        copy.wait()
    wide_ref[...] = inputs_ref[...].astype(F32)
    consts_ref[0:1, :] = start_ref[...]
    consts_ref[1:2, :] = rec_bias_ref[...]
    consts_ref[2:, :] = jnp.zeros((6, units), F32)


def own_kernel(
    own_ref, consts_ref, in_weight_ref, bias_ref, weight_ref,
    gates_ref, mats_ref, vecs_ref, prev_ref, *coef_refs
):
    share, units = own_ref.shape
    gates = jnp.dot(own_ref[...].astype(BF16), in_weight_ref[...], preferred_element_type=F32) + bias_ref[...]
    gates_ref[...] = gates
    at_start = (lax.axis_index("tm") == 0) & (lax.broadcasted_iota(jnp.int32, (share, units), 0) == 0)
    previous = jnp.where(at_start, consts_ref[0:1, :], 0.0)
    prev_ref[...] = previous
    parts = cell(gates, previous, weight_ref[...], consts_ref[1:2, :])
    fold(parts, prev_ref, weight_ref, coef_refs, [0], slots_in([mats_ref, vecs_ref]), share)


def first_kernel(
    at_front, whole, consts_ref, in_weight_ref, bias_ref, weight_ref, own_gates_ref, own_mats_ref, own_vecs_ref, *refs
):
    shares, refs = refs[: SPAN - 1], refs[SPAN - 1 :]
    gates_ref, sums_ref, prev_ref, top_mats, top_vecs, mats_ref, vecs_ref, sent_ref, map_ref, *scratch = refs
    top_scratch, coef_refs = scratch[:2], scratch[2:]
    steps, units = prev_ref.shape
    share = steps // SPAN

    @pl.when((group() == 0) == at_front)
    def _():
        sums_ref[...] = jnp.zeros(sums_ref.shape, F32)
        inputs = jnp.concatenate([one[...] for one in shares], axis=0).astype(BF16)
        gates = jnp.dot(inputs, in_weight_ref[...], preferred_element_type=F32) + bias_ref[...]
        gates_ref[:share, :] = own_gates_ref[...]
        gates_ref[share:, :] = gates
        previous = jnp.zeros((steps, units), F32)
        if at_front:
            row = lax.broadcasted_iota(jnp.int32, (steps, units), 0)
            previous = jnp.where(row == slot_of(0) * share, consts_ref[0:1, :], 0.0)
        prev_ref[...] = previous
        parts = cell(gates, previous[share:], weight_ref[...], consts_ref[1:2, :])
        pieces = slots_in([own_mats_ref, own_vecs_ref, mats_ref, vecs_ref])
        fold(parts, prev_ref, weight_ref, coef_refs, list(range(1, SPAN)), pieces, share)
        fold_shares(prev_ref, pieces, share, (top_mats, top_vecs), top_scratch, map_ref, whole)
        if at_front:
            send_on(consts_ref[0:1, :], map_ref, sent_ref)


def hop_kernel(sent_first_ref, map_ref, arrived_ref, sent_ref):
    state = through(arrived_ref[0:1, :], map_ref)
    sent_ref[...] = jnp.where(group() == 0, sent_first_ref[...], state)


def middle_kernel(
    newton, at_front, whole, held, start_ref, consts_ref, weight_ref, gates_ref, sums_ref, old_prev_ref, *refs
):
    old_tops, old, refs = refs[:2], refs[2:held], refs[held:]
    new_sums_ref, new_prev_ref, top_mats, top_vecs, mats_ref, vecs_ref, sent_ref, map_ref, *scratch = refs
    states_ref, starts_ref, top_scratch, coef_refs = scratch[0], scratch[1], scratch[2:4], scratch[4:]
    share = states_ref.shape[0] // SPAN

    @pl.when((group() == 0) == at_front)
    def _():
        entering = start_ref[0:1, :]
        unfold(entering, old_prev_ref, slots_in(old), old_tops, share, starts_ref, states_ref)
        shift_in(starts_ref, states_ref, new_prev_ref, share)
        parts = cell(gates_ref[...], new_prev_ref[...], weight_ref[...], consts_ref[1:2, :])
        add_sum(newton, sums_ref, states_ref, parts, new_sums_ref)
        pieces = slots_in([mats_ref, vecs_ref])
        fold(parts, new_prev_ref, weight_ref, coef_refs, list(range(SPAN)), pieces, share)
        fold_shares(new_prev_ref, pieces, share, (top_mats, top_vecs), top_scratch, map_ref, whole)
        if at_front:
            send_on(entering, map_ref, sent_ref)


def add_sum(newton, sums_ref, states_ref, parts, new_sums_ref):
    done = weighted_square(states_ref[...], parts[4])
    lane = lax.broadcasted_iota(jnp.int32, new_sums_ref.shape, 1)
    new_sums_ref[...] = jnp.where(lane == newton, done, sums_ref[...])


def last_kernel(newton, sides, held, consts_ref, weight_ref, *refs):
    sides_refs, refs = [refs[held * i : held * i + held] for i in range(sides)], refs[held * sides :]
    out_ref, new_sums_ref, prev_ref, states_ref, starts_ref = refs
    share = out_ref.shape[0]
    for side, (start_ref, gates_ref, sums_ref, old_prev_ref, *old) in enumerate(sides_refs):

        @pl.when((group() == 0) == (side == 0))
        def _():
            unfold(start_ref[0:1, :], old_prev_ref, slots_in(old[2:]), old[:2], share, starts_ref, states_ref)
            shift_in(starts_ref, states_ref, prev_ref, share)
            parts = cell(gates_ref[...], prev_ref[...], weight_ref[...], consts_ref[1:2, :])
            add_sum(newton, sums_ref, states_ref, parts, new_sums_ref)

    out_ref[...] = states_ref[:share, :]


def call(kernel, args, outs, scratch=(), space=pltpu.VMEM):
    args = [pltpu.with_memory_space_constraint(arg, space) for arg in args]
    return pl.pallas_call(
        kernel,
        out_shape=[jax.ShapeDtypeStruct(o, F32) if isinstance(o, tuple) else o for o in outs],
        in_specs=[pl.BlockSpec(memory_space=space)] * len(args),
        out_specs=[pl.BlockSpec(memory_space=pltpu.VMEM)] * len(outs),
        scratch_shapes=[pltpu.VMEM(one, F32) if isinstance(one, tuple) else one for one in scratch],
        compiler_params=pltpu.CompilerParams(vmem_limit_bytes=16 * 1024 * 1024),
    )(*args)


def exchanged(value, axis, by):
    return lax.ppermute(value, axis, [(i, i ^ by) for i in range(lax.axis_size(axis))])


def summed(value, axis, by=1):
    count = lax.axis_size(axis)
    while by < count:
        radix = min(4, count // by)
        terms = [value] + [exchanged(value, axis, k * by) for k in range(1, radix)]
        while len(terms) > 1:
            terms = [a + b for a, b in zip(terms[0::2], terms[1::2])]
        value = terms[0]
        by *= radix
    return value


def carry(sent, own_map):
    count = lax.axis_size("tm")
    onward = [(i, i + SPAN) for i in range(count - SPAN)]
    arrived = lax.ppermute(sent, "tm", onward)
    for _ in range(count // SPAN - 2):
        (further,) = call(hop_kernel, [sent, *own_map, arrived], [sent.shape])
        arrived = lax.ppermute(further, "tm", onward)
    return arrived


def per_device(
    inputs, h_start, in_weight, rec_weight, update_bias, reset_bias, cand_bias, rec_bias
):
    share, sequences = inputs.shape[0], inputs.shape[1]
    units = rec_weight.shape[0]
    row = lambda value: value.reshape(1, units)
    steps = share * SPAN
    rows, wide = (steps, units), (steps, 3 * units)
    sides = min(2, lax.axis_size("tm") // SPAN)
    slots = layout(share)[1]
    of_slots = lambda count: [(count, slots, units, units), (count, slots, units)]
    tops = [(8, units, units), (8, units)]
    top_scratch = [(SPAN, units, units), (8, units)]
    state_row, map_rows = (8, units), (units + 8, units)
    further = lax.axis_size("tm") // SPAN > 2
    ends = [([state_row], [map_rows])]
    if sides > 1:
        ends.append(([state_row, map_rows], []) if further else ([], [state_row, map_rows]))
    own, in_rows, weight, bias, consts = call(
        fetch_kernel,
        [inputs.reshape(share, -1), h_start, in_weight, rec_weight, row(update_bias), row(reset_bias),
         row(cand_bias), row(rec_bias)],
        [(share, units), jax.ShapeDtypeStruct(in_weight.shape, BF16), rec_weight.shape, (1, 3 * units),
         (8, units)],
        [pltpu.VMEM((share, units), BF16), (1, units), (1, units), pltpu.SemaphoreType.DMA((8,))],
        space=pltpu.HBM,
    )
    shares = [exchanged(own, "tm", k) for k in range(1, SPAN)]
    own_gates, *own_slot = call(
        own_kernel, [own, consts, in_rows, bias, weight], [(share, 3 * units)] + of_slots(1),
        [(share, units)] * 6,
    )
    held = []
    beside = []
    for side, (out, kept) in enumerate(ends):
        gates, sums, prev, top_mats, top_vecs, mats, vecs, *more = call(
            functools.partial(first_kernel, side == 0, side == 0 or further),
            [consts, in_rows, bias, weight, own_gates, *own_slot, *shares],
            [wide, (8, units), rows] + tops + of_slots(SPAN - 1) + out,
            kept + top_scratch + [(steps - share, units)] * 5,
        )
        held.append([gates, sums, prev, top_mats, top_vecs, *own_slot, mats, vecs])
        beside.append(more)
    for newton in range(ITERS):
        starts = [consts] + [carry(beside[0][0], beside[-1][1:])] * (sides - 1)
        if newton < ITERS - 1:
            for side, (out, kept) in enumerate(ends):
                solved = call(
                    functools.partial(
                        middle_kernel, newton, side == 0, side == 0 or further, len(held[side]) - 3
                    ),
                    [starts[side], consts, weight, *held[side]],
                    [(8, units), rows] + tops + of_slots(SPAN) + out,
                    kept + [rows, (8, units)] + top_scratch + [rows] * 5,
                )
                held[side] = [held[side][0], *solved[:6]]
                beside[side] = solved[6:]
        else:
            args = [one for side in range(sides) for one in (starts[side], *held[side])]
            states, total = call(
                functools.partial(last_kernel, newton, sides, len(held[0]) + 1), [consts, weight, *args],
                [(share, units), (8, units)], [rows, rows, (8, units)],
            )
    totals = summed(summed(total, "batch"), "tm", SPAN)[0, :ITERS]
    denom = lax.axis_size("batch") * sequences * units * (share * lax.axis_size("tm") + 1) / 2.0
    residual_norms = jnp.sqrt(totals / denom + 1e-06)
    return (states.reshape(share, sequences, units), residual_norms)


def solution(mesh):
    in_specs = (P("tm", "batch", None), P("batch", None), P(), P(), P(), P(), P(), P())
    out_specs = (P("tm", "batch", None), P())
    return jax.shard_map(
        per_device, mesh=mesh, in_specs=in_specs, out_specs=out_specs, check_vma=False
    )
```

```python
import functools

import jax
import jax.numpy as jnp
from jax import lax
from jax.experimental import pallas as pl
from jax.experimental.pallas import tpu as pltpu
from jax.sharding import PartitionSpec as P

ITERS = 2
SPAN = 4
SIZE = 8
PAD = 16
F32 = jnp.float32
BF16 = jnp.bfloat16


def halves(value):
    high = value.astype(BF16)
    return high, (value - high.astype(F32)).astype(BF16)


def paired_rows(value):
    return jnp.concatenate(halves(value), axis=1)


def paired_cols(value):
    both = jnp.concatenate(halves(value), axis=1)
    return jnp.concatenate([both, both], axis=0)


def product(rows, cols):
    width = cols.shape[1]
    both = jnp.dot(paired_rows(rows), paired_cols(cols), preferred_element_type=F32)
    return both[:, :width] + both[:, width:]


def as_column(row):
    units = row.shape[1]
    return jnp.broadcast_to(row, (units, units)).T


def row_times(column, matrix):
    return jnp.sum(column * matrix, axis=0, keepdims=True)


def cell(gates, previous, rec_weight, rec_bias):
    units = previous.shape[1]
    rec = product(previous, rec_weight)
    update = jax.nn.sigmoid(gates[:, :units] + rec[:, :units])
    reset = jax.nn.sigmoid(gates[:, units : 2 * units] + rec[:, units : 2 * units])
    recur = rec[:, 2 * units :] + rec_bias
    cand = jnp.tanh(gates[:, 2 * units :] + reset * recur)
    stepped = (1.0 - update) * cand + update * previous
    return update, reset, recur, cand, stepped


def group():
    return lax.axis_index("tm") // SPAN


def through(state, one_map):
    units = state.shape[1]
    column = as_column(state - one_map[units + 1 : units + 2, :])
    return row_times(column, one_map[:units, :]) + one_map[units : units + 1, :]


def stacked(mat, vec):
    return jnp.concatenate([mat, jnp.broadcast_to(vec, (PAD, mat.shape[1]))], axis=0)


def join(mats, vecs, early, late, base, out):
    after = product(stacked(mats[early], vecs[early : early + 1, :] - base), mats[late])
    units = after.shape[1]
    mats[out] = after[:units]
    vecs[out : out + 1, :] = after[units : units + 1] + vecs[late : late + 1, :]


def layout(share):
    blocks = share // SIZE
    where = {(b, 1): (b + 1) * SIZE - 1 for b in range(blocks)}
    free, span = share, 2
    while span <= blocks:
        for b in range(0, blocks, span):
            where[(b, span)] = free
            free += 1
        span *= 2
    return where, -(-free // 8) * 8


def fold(parts, prev_ref, weight_ref, coef_refs, slots, pieces, share):
    update, reset, recur, cand, stepped = parts
    units = update.shape[1]
    previous = prev_ref[slots[0] * share : (slots[-1] + 1) * share, :]
    update_ref, coef_update_ref, coef_reset_ref, coef_cand_ref, step_ref = coef_refs
    common = (1.0 - update) * (1.0 - cand * cand)
    update_ref[...] = update
    coef_update_ref[...] = (previous - cand) * update * (1.0 - update)
    coef_reset_ref[...] = common * recur * reset * (1.0 - reset)
    coef_cand_ref[...] = common * reset
    step_ref[...] = stepped
    row = lax.broadcasted_iota(jnp.int32, (units, units), 0)
    col = lax.broadcasted_iota(jnp.int32, (units, units), 1)

    def slope(r):
        return (
            weight_ref[:, :units] * coef_update_ref[r : r + 1, :]
            + weight_ref[:, units : 2 * units] * coef_reset_ref[r : r + 1, :]
            + weight_ref[:, 2 * units :] * coef_cand_ref[r : r + 1, :]
        )

    for inner in range(SIZE):
        for i, k in enumerate(slots):
            mats, vecs = pieces[k]
            for t in range(inner, share, SIZE):
                r = i * share + t
                if inner == 0:
                    mats[t] = slope(r) + jnp.where(row == col, update_ref[r : r + 1, :], 0.0)
                    vecs[t : t + 1, :] = step_ref[r : r + 1, :]
                    continue
                taken = prev_ref[k * share + t : k * share + t + 1, :]
                before = stacked(mats[t - 1], vecs[t - 1 : t, :] - taken)
                after = product(before, slope(r)) + before * update_ref[r : r + 1, :]
                mats[t] = after[:units]
                vecs[t : t + 1, :] = after[units : units + 1] + step_ref[r : r + 1, :]
    where, _ = layout(share)
    for (b, span), out in where.items():
        if span > 1:
            second = b + span // 2
            for k in slots:
                base = prev_ref[k * share + second * SIZE : k * share + second * SIZE + 1, :]
                join(*pieces[k], where[(b, span // 2)], where[(second, span // 2)], base, out)


def share_map(share):
    return layout(share)[0][(0, share // SIZE)]


def slot_of(part):
    return lax.rem(lax.axis_index("tm"), SPAN) ^ part


def base_of(prev_ref, part, share):
    return prev_ref[pl.ds(slot_of(part) * share, 1), :]


def fold_shares(prev_ref, pieces, share, tops, top_scratch, map_ref, whole):
    mats, vecs = tops
    held_mats, held_vecs = top_scratch
    at = share_map(share)
    for k in range(SPAN):
        held_mats[k] = pieces[k][0][at]
        held_vecs[k : k + 1, :] = pieces[k][1][at : at + 1, :]
    for part in range(SPAN):
        mats[part] = held_mats[slot_of(part)]
        vecs[part : part + 1, :] = held_vecs[pl.ds(slot_of(part), 1), :]
    join(mats, vecs, 0, 1, base_of(prev_ref, 1, share), 4)
    if whole:
        units = map_ref.shape[1]
        join(mats, vecs, 2, 3, base_of(prev_ref, 3, share), 5)
        join(mats, vecs, 4, 5, base_of(prev_ref, 2, share), 6)
        map_ref[:units, :] = mats[6]
        map_ref[units : units + 1, :] = vecs[6:7, :]
        map_ref[units + 1 : units + 2, :] = base_of(prev_ref, 0, share)
        map_ref[units + 2 :, :] = jnp.zeros((6, units), F32)


def unfold(entering, prev_ref, pieces, tops, share, starts_ref, out_ref):
    top_mats, top_vecs = tops
    starts_ref[0:1, :] = entering
    column = as_column(entering - base_of(prev_ref, 0, share))
    middle = row_times(column, top_mats[4]) + top_vecs[4:5, :]
    starts_ref[1:2, :] = row_times(column, top_mats[0]) + top_vecs[0:1, :]
    starts_ref[2:3, :] = middle
    column = as_column(middle - base_of(prev_ref, 2, share))
    starts_ref[3:4, :] = row_times(column, top_mats[2]) + top_vecs[2:3, :]
    where, _ = layout(share)
    blocks = share // SIZE
    starts = {(0, k): starts_ref[pl.ds(slot_of(k), 1), :] for k in range(SPAN)}
    for b in sorted(range(blocks), key=lambda b: (bin(b).count("1"), -b)):
        for k in range(SPAN):
            mats, vecs = pieces[k]
            t, first = b * SIZE, k * share + b * SIZE
            column = as_column(starts[(b, k)] - prev_ref[first : first + 1, :])
            span = 1
            while b % (2 * span) == 0 and b + span < blocks:
                at = where[(b, span)]
                starts[(b + span, k)] = row_times(column, mats[at]) + vecs[at : at + 1, :]
                span *= 2
            for inner in range(SIZE):
                state = row_times(column, mats[t + inner]) + vecs[t + inner : t + inner + 1, :]
                out_ref[first + inner : first + inner + 1, :] = state


def shift_in(starts_ref, states_ref, prev_ref, share):
    steps = states_ref.shape[0]
    prev_ref[1:steps, :] = states_ref[0 : steps - 1, :]
    for k in range(SPAN):
        prev_ref[k * share : k * share + 1, :] = starts_ref[pl.ds(slot_of(k), 1), :]


def slots_in(refs):
    return [(mats.at[k], vecs.at[k]) for mats, vecs in zip(refs[0::2], refs[1::2]) for k in range(mats.shape[0])]


def weighted_square(states, stepped):
    steps = states.shape[0]
    share = steps // SPAN
    count = lax.axis_size("tm") // SPAN
    row = lax.broadcasted_iota(jnp.int32, states.shape, 0)
    position = group() * steps + slot_of(row // share) * share + row % share
    weights = (position.astype(F32) + 1.0) / (steps * count)
    return jnp.sum(weights * (states - stepped) ** 2, axis=(0, 1), keepdims=True)


def send_on(start, map_ref, sent_ref):
    sent_ref[...] = jnp.broadcast_to(through(start, map_ref), sent_ref.shape)


def fetch_kernel(
    inputs_hbm, start_hbm, in_weight_hbm, weight_hbm, update_bias_hbm, reset_bias_hbm, cand_bias_hbm,
    rec_bias_hbm,
    wide_ref, in_weight_ref, weight_ref, bias_ref, consts_ref,
    inputs_ref, start_ref, rec_bias_ref, sems
):
    units = weight_ref.shape[0]
    moves = [
        (inputs_hbm, inputs_ref), (in_weight_hbm, in_weight_ref), (weight_hbm, weight_ref),
        (update_bias_hbm, bias_ref.at[:, pl.ds(0, units)]),
        (reset_bias_hbm, bias_ref.at[:, pl.ds(units, units)]),
        (cand_bias_hbm, bias_ref.at[:, pl.ds(2 * units, units)]),
        (start_hbm, start_ref), (rec_bias_hbm, rec_bias_ref),
    ]
    copies = [pltpu.make_async_copy(src, dst, sems.at[i]) for i, (src, dst) in enumerate(moves)]
    for copy in copies:
        copy.start()
    for copy in copies:
        copy.wait()
    wide_ref[...] = inputs_ref[...].astype(F32)
    consts_ref[0:1, :] = start_ref[...]
    consts_ref[1:2, :] = rec_bias_ref[...]
    consts_ref[2:, :] = jnp.zeros((6, units), F32)


def own_kernel(
    own_ref, consts_ref, in_weight_ref, bias_ref, weight_ref,
    gates_ref, mats_ref, vecs_ref, prev_ref, *coef_refs
):
    share, units = own_ref.shape
    gates = jnp.dot(own_ref[...].astype(BF16), in_weight_ref[...], preferred_element_type=F32) + bias_ref[...]
    gates_ref[...] = gates
    at_start = (lax.axis_index("tm") == 0) & (lax.broadcasted_iota(jnp.int32, (share, units), 0) == 0)
    previous = jnp.where(at_start, consts_ref[0:1, :], 0.0)
    prev_ref[...] = previous
    parts = cell(gates, previous, weight_ref[...], consts_ref[1:2, :])
    fold(parts, prev_ref, weight_ref, coef_refs, [0], slots_in([mats_ref, vecs_ref]), share)


def first_kernel(
    at_front, whole, consts_ref, in_weight_ref, bias_ref, weight_ref, own_gates_ref, own_mats_ref, own_vecs_ref, *refs
):
    shares, refs = refs[: SPAN - 1], refs[SPAN - 1 :]
    gates_ref, sums_ref, prev_ref, top_mats, top_vecs, mats_ref, vecs_ref, sent_ref, map_ref, *scratch = refs
    top_scratch, coef_refs = scratch[:2], scratch[2:]
    steps, units = prev_ref.shape
    share = steps // SPAN

    @pl.when((group() == 0) == at_front)
    def _():
        sums_ref[...] = jnp.zeros(sums_ref.shape, F32)
        inputs = jnp.concatenate([one[...] for one in shares[::-1]], axis=0).astype(BF16)
        gates = jnp.dot(inputs, in_weight_ref[...], preferred_element_type=F32) + bias_ref[...]
        gates_ref[:share, :] = own_gates_ref[...]
        gates_ref[share:, :] = gates
        previous = jnp.zeros((steps, units), F32)
        if at_front:
            row = lax.broadcasted_iota(jnp.int32, (steps, units), 0)
            previous = jnp.where(row == slot_of(0) * share, consts_ref[0:1, :], 0.0)
        prev_ref[...] = previous
        parts = cell(gates, previous[share:], weight_ref[...], consts_ref[1:2, :])
        pieces = slots_in([own_mats_ref, own_vecs_ref, mats_ref, vecs_ref])
        fold(parts, prev_ref, weight_ref, coef_refs, list(range(1, SPAN)), pieces, share)
        fold_shares(prev_ref, pieces, share, (top_mats, top_vecs), top_scratch, map_ref, whole)
        if at_front:
            send_on(consts_ref[0:1, :], map_ref, sent_ref)


def hop_kernel(sent_first_ref, map_ref, arrived_ref, sent_ref):
    state = through(arrived_ref[0:1, :], map_ref)
    sent_ref[...] = jnp.where(group() == 0, sent_first_ref[...], state)


def middle_kernel(
    newton, at_front, whole, held, start_ref, consts_ref, weight_ref, gates_ref, sums_ref, old_prev_ref, *refs
):
    old_tops, old, refs = refs[:2], refs[2:held], refs[held:]
    new_sums_ref, new_prev_ref, top_mats, top_vecs, mats_ref, vecs_ref, sent_ref, map_ref, *scratch = refs
    states_ref, starts_ref, top_scratch, coef_refs = scratch[0], scratch[1], scratch[2:4], scratch[4:]
    share = states_ref.shape[0] // SPAN

    @pl.when((group() == 0) == at_front)
    def _():
        entering = start_ref[0:1, :]
        unfold(entering, old_prev_ref, slots_in(old), old_tops, share, starts_ref, states_ref)
        shift_in(starts_ref, states_ref, new_prev_ref, share)
        parts = cell(gates_ref[...], new_prev_ref[...], weight_ref[...], consts_ref[1:2, :])
        add_sum(newton, sums_ref, states_ref, parts, new_sums_ref)
        pieces = slots_in([mats_ref, vecs_ref])
        fold(parts, new_prev_ref, weight_ref, coef_refs, list(range(SPAN)), pieces, share)
        fold_shares(new_prev_ref, pieces, share, (top_mats, top_vecs), top_scratch, map_ref, whole)
        if at_front:
            send_on(entering, map_ref, sent_ref)


def add_sum(newton, sums_ref, states_ref, parts, new_sums_ref):
    done = weighted_square(states_ref[...], parts[4])
    lane = lax.broadcasted_iota(jnp.int32, new_sums_ref.shape, 1)
    new_sums_ref[...] = jnp.where(lane == newton, done, sums_ref[...])


def last_kernel(newton, at_front, held, start_ref, consts_ref, weight_ref, *refs):
    (gates_ref, sums_ref, old_prev_ref, *old), refs = refs[:held], refs[held:]
    *front, out_ref, new_sums_ref, prev_ref, states_ref, starts_ref = refs
    share = out_ref.shape[0]

    @pl.when((group() == 0) == at_front)
    def _():
        unfold(start_ref[0:1, :], old_prev_ref, slots_in(old[2:]), old[:2], share, starts_ref, states_ref)
        shift_in(starts_ref, states_ref, prev_ref, share)
        parts = cell(gates_ref[...], prev_ref[...], weight_ref[...], consts_ref[1:2, :])
        add_sum(newton, sums_ref, states_ref, parts, new_sums_ref)
        out_ref[...] = states_ref[:share, :]

    if not at_front:

        @pl.when(group() == 0)
        def _():
            out_ref[...] = front[0][...]
            new_sums_ref[...] = front[1][...]


def call(kernel, args, outs, scratch=(), space=pltpu.VMEM):
    args = [pltpu.with_memory_space_constraint(arg, space) for arg in args]
    return pl.pallas_call(
        kernel,
        out_shape=[jax.ShapeDtypeStruct(o, F32) if isinstance(o, tuple) else o for o in outs],
        in_specs=[pl.BlockSpec(memory_space=space)] * len(args),
        out_specs=[pl.BlockSpec(memory_space=pltpu.VMEM)] * len(outs),
        scratch_shapes=[pltpu.VMEM(one, F32) if isinstance(one, tuple) else one for one in scratch],
        compiler_params=pltpu.CompilerParams(vmem_limit_bytes=16 * 1024 * 1024),
    )(*args)


def exchanged(value, axis, by):
    return lax.ppermute(value, axis, [(i, i ^ by) for i in range(lax.axis_size(axis))])


def summed(value, axis, by=1):
    count = lax.axis_size(axis)
    while by < count:
        radix = min(4, count // by)
        terms = [exchanged(value, axis, k * by) for k in range(radix - 1, 0, -1)] + [value]
        while len(terms) > 1:
            terms = [a + b for a, b in zip(terms[0::2], terms[1::2])]
        value = terms[0]
        by *= radix
    return value


def carry(sent, own_map):
    count = lax.axis_size("tm")
    onward = [(i, i + SPAN) for i in range(count - SPAN)]
    arrived = lax.ppermute(sent, "tm", onward)
    for _ in range(count // SPAN - 2):
        (further,) = call(hop_kernel, [sent, *own_map, arrived], [sent.shape])
        arrived = lax.ppermute(further, "tm", onward)
    return arrived


def per_device(
    inputs, h_start, in_weight, rec_weight, update_bias, reset_bias, cand_bias, rec_bias
):
    share, sequences = inputs.shape[0], inputs.shape[1]
    units = rec_weight.shape[0]
    row = lambda value: value.reshape(1, units)
    steps = share * SPAN
    rows, wide = (steps, units), (steps, 3 * units)
    sides = min(2, lax.axis_size("tm") // SPAN)
    slots = layout(share)[1]
    of_slots = lambda count: [(count, slots, units, units), (count, slots, units)]
    tops = [(8, units, units), (8, units)]
    top_scratch = [(SPAN, units, units), (8, units)]
    state_row, map_rows = (8, units), (units + 8, units)
    further = lax.axis_size("tm") // SPAN > 2
    ends = [([state_row], [map_rows])]
    if sides > 1:
        ends.append(([state_row, map_rows], []) if further else ([], [state_row, map_rows]))
    own, in_rows, weight, bias, consts = call(
        fetch_kernel,
        [inputs.reshape(share, -1), h_start, in_weight, rec_weight, row(update_bias), row(reset_bias),
         row(cand_bias), row(rec_bias)],
        [(share, units), jax.ShapeDtypeStruct(in_weight.shape, BF16), rec_weight.shape, (1, 3 * units),
         (8, units)],
        [pltpu.VMEM((share, units), BF16), (1, units), (1, units), pltpu.SemaphoreType.DMA((8,))],
        space=pltpu.HBM,
    )
    shares = [exchanged(own, "tm", k) for k in range(SPAN - 1, 0, -1)]
    own_gates, *own_slot = call(
        own_kernel, [own, consts, in_rows, bias, weight], [(share, 3 * units)] + of_slots(1),
        [(share, units)] * 6,
    )
    held = []
    beside = []
    for side, (out, kept) in enumerate(ends):
        gates, sums, prev, top_mats, top_vecs, mats, vecs, *more = call(
            functools.partial(first_kernel, side == 0, side == 0 or further),
            [consts, in_rows, bias, weight, own_gates, *own_slot, *shares],
            [wide, (8, units), rows] + tops + of_slots(SPAN - 1) + out,
            kept + top_scratch + [(steps - share, units)] * 5,
        )
        held.append([gates, sums, prev, top_mats, top_vecs, *own_slot, mats, vecs])
        beside.append(more)
    for newton in range(ITERS):
        starts = [consts] + [carry(beside[0][0], beside[-1][1:])] * (sides - 1)
        if newton < ITERS - 1:
            for side, (out, kept) in enumerate(ends):
                solved = call(
                    functools.partial(
                        middle_kernel, newton, side == 0, side == 0 or further, len(held[side]) - 3
                    ),
                    [starts[side], consts, weight, *held[side]],
                    [(8, units), rows] + tops + of_slots(SPAN) + out,
                    kept + [rows, (8, units)] + top_scratch + [rows] * 5,
                )
                held[side] = [held[side][0], *solved[:6]]
                beside[side] = solved[6:]
        else:
            solved = []
            for side in range(sides):
                solved.append(call(
                    functools.partial(last_kernel, newton, side == 0, len(held[side])),
                    [starts[side], consts, weight, *held[side], *(solved[0] if side else [])],
                    [(share, units), (8, units)], [rows, rows, (8, units)],
                ))
            states, total = solved[-1]
    if sides > 1 and not further:
        ahead = [(i, i + SPAN) for i in range(SPAN)]
        to_others = lax.ppermute(solved[0][1], "tm", ahead)
        to_first = lax.ppermute(total, "tm", [(j, i) for i, j in ahead])
        total = total + (to_others + to_first)
    elif further:
        total = summed(total, "tm", SPAN)
    totals = summed(total, "batch")[0, :ITERS]
    denom = lax.axis_size("batch") * sequences * units * (share * lax.axis_size("tm") + 1) / 2.0
    residual_norms = jnp.sqrt(totals / denom + 1e-06)
    return (states.reshape(share, sequences, units), residual_norms)


def solution(mesh):
    in_specs = (P("tm", "batch", None), P("batch", None), P(), P(), P(), P(), P(), P())
    out_specs = (P("tm", "batch", None), P())
    return jax.shard_map(
        per_device, mesh=mesh, in_specs=in_specs, out_specs=out_specs, check_vma=False
    )
```
